256 devices in a mesh: dp: 64 (over z, y, core), mp: 4 (over x).
Axes of the slice: x: 4, y: 4, z: 8, core: 2. Of those that a mesh axis runs over, the one named last changes fastest.
Arguments:
- texts: bfloat16 [1536, 128, 1024], P('dp')
- w_qkv: bfloat16 [1024, 3072], P(None, 'mp'), may hold values from -0.1875 to 0.1875
- w_out: bfloat16 [1024, 1024], P('mp'), may hold values from -0.75 to 0.75
- w_self: bfloat16 [1024, 1024], P('mp'), may hold values from -0.1875 to 0.1875
- w_neigh: bfloat16 [1024, 1024], P('mp'), may hold values from -0.1875 to 0.1875
- neighbours: int32 [1536, 16], P('dp'), may hold values from -1 to 1535, as said below
- cotangent: bfloat16 [1536, 1024], P('dp', 'mp'), may hold values from -6 to 6
Outputs:
- mixed: bfloat16 [1536, 1024], P('dp', 'mp')
- node_grad: bfloat16 [1536, 1024], P('dp', 'mp')
- grad_w_self: float32 [1024, 1024], P('mp')
- grad_w_neigh: float32 [1024, 1024], P('mp')
- grad_w_out: float32 [1024, 1024], P('mp')
The draws below stay inside these ranges and needn't reach their ends.
Inputs may be any that keep to these rules, and one draw needn't show every extreme that they name: `neighbours`: A node id j lives with index j // 24 of dp. In the rows of one dp device (aligned blocks of 24 rows) at most 6 entries fall in any one owner's id range, and some owner gets exactly 6; entries are -1 or ids below 1536. Some targets have every slot -1.
All inputs are finite; a program needn't handle non-finite values.
Results may differ from the reference program's by a relative error of at most 0.029.
The reference program's roundings to bfloat16 on the way (of `qkv`, `probs`, `pooled`, `embed`, `agg`, `dz` and `msg`) count: a program that leaves them out, or rounds other values in their place, can miss the bound.
Values may be sent and summed in bfloat16 or wider, within the bound.
A program may use at most 64 MiB of HBM per device.

```python
import jax
import jax.numpy as jnp
from jax import lax

D = 1024
HEADS = 16
HD = 64
L = 128
FAN = 16
NODE_DEV = 24
NODES = 1536


def draw_texts(key, part):
    key = jax.random.fold_in(key, 5)
    first = jax.random.fold_in(key, 0)
    base = jax.random.normal(first, (NODES, L, D), jnp.float32)
    return base.astype(jnp.bfloat16)


def draw_neighbours(key, part):
    key = jax.random.fold_in(key, 11)
    groups = NODES // NODE_DEV
    slots = NODE_DEV * FAN
    limit = slots // groups
    room = slots - FAN

    def one_group(gkey):
        k_count, k_full, k_local, k_order, k_empty = jax.random.split(gkey, 5)
        counts = jax.random.randint(k_count, (groups,), 0, limit + 1)
        full_owner = jax.random.randint(k_full, (), 0, groups)
        counts = jnp.where(jnp.arange(groups) == full_owner, limit, counts)
        rotated = (jnp.arange(groups) + full_owner) % groups
        counts_rot = counts[rotated]
        before = jnp.cumsum(counts_rot) - counts_rot
        kept_rot = jnp.clip(room - before, 0, counts_rot)
        kept = jnp.zeros((groups,), jnp.int32).at[rotated].set(kept_rot.astype(jnp.int32))
        slot = jnp.arange(slots)
        owner = slot // limit
        rank = slot % limit
        local = jax.random.randint(k_local, (slots,), 0, NODE_DEV)
        ids = jnp.where(rank < kept[owner], owner * NODE_DEV + local, -1)
        live_first = jnp.argsort((ids < 0).astype(jnp.int32) * slots + slot, stable=True)
        packed = ids[live_first]
        empty_row = jax.random.randint(k_empty, (), 0, NODE_DEV)
        shuffled = jax.random.permutation(k_order, slots)
        in_empty = (shuffled // FAN == empty_row).astype(jnp.int32)
        places = shuffled[jnp.argsort(in_empty * slots + slot, stable=True)]
        result = jnp.full((slots,), -1, jnp.int32).at[places].set(packed.astype(jnp.int32))
        return result.reshape(NODE_DEV, FAN)
    group_keys = jax.random.split(key, groups)
    return jax.vmap(one_group)(group_keys).reshape(NODES, FAN).astype(jnp.int32)


def block_levels(key, extent, pieces, low, top_value):
    level, own = 1.0, jax.random.fold_in(key, 6)
    for axis_at, parts in pieces:
        heights = jnp.exp(jax.random.uniform(jax.random.fold_in(own, axis_at), (parts,), jnp.float32, low / len(pieces), top_value / len(pieces)))
        level = level * jnp.repeat(heights, extent[axis_at] // parts).reshape([-1 if axis == axis_at else 1 for axis in range(len(extent))])
    return level


def centred(key, shape, width, most, pieces=(), kind=jnp.bfloat16):
    factor_of = block_levels(key, shape, pieces, -0.22, 0.18) if pieces else 1.0
    entries = jax.random.normal(key, shape, jnp.float32) * width * factor_of
    return jnp.minimum(jnp.maximum(entries, -most), most).astype(kind)


def setup_inputs(seed: int = 0) -> dict:
    splits = jax.random.split(jax.random.key(seed), 8)
    return {
        "texts": draw_texts(jax.random.fold_in(splits[7], 71), 0),
        "w_qkv": centred(splits[1], (D, 3 * D), D ** -0.5, 0.1875, ((1, 4),)),
        "w_out": centred(splits[2], (D, D), HD ** -0.5, 0.75, ((0, 4),)),
        "w_self": centred(splits[3], (D, D), D ** -0.5, 0.1875, ((0, 4),)),
        "w_neigh": centred(splits[4], (D, D), D ** -0.5, 0.1875, ((0, 4),)),
        "neighbours": draw_neighbours(jax.random.fold_in(splits[7], 71), 0),
        "cotangent": centred(splits[6], (NODES, D), 1.0, 6.0, ((0, 64), (1, 4))),
    }


def encode_block(block, w_qkv):
    count = block.shape[0]
    qkv = jnp.einsum('nld,de->nle', block.astype(jnp.float32), w_qkv.astype(jnp.float32)).astype(jnp.bfloat16)
    qkv = qkv.reshape(count, L, HEADS, 3, HD)
    query = qkv[:, :, :, 0, :].astype(jnp.float32)
    keys = qkv[:, :, :, 1, :].astype(jnp.float32)
    values = qkv[:, :, :, 2, :].astype(jnp.float32)
    scores = jnp.einsum('nqhd,nkhd->nhqk', query, keys) / jnp.sqrt(jnp.float32(HD))
    probs = jax.nn.softmax(scores, axis=-1).astype(jnp.bfloat16)
    context = jnp.einsum('nhqk,nkhd->nhd', probs.astype(jnp.float32), values) / jnp.float32(L)
    return context.reshape(count, D).astype(jnp.bfloat16)

def reference(texts, w_qkv, w_out, w_self, w_neigh, neighbours, cotangent):
    blocks = texts.reshape(NODES // 8, 8, L, D)
    pooled = lax.map(lambda blk: encode_block(blk, w_qkv), blocks).reshape(NODES, D)
    token_mean = lax.optimization_barrier(jnp.mean(texts.astype(jnp.float32), axis=1))
    embed = (token_mean + jnp.dot(pooled, w_out, preferred_element_type=jnp.float32)).astype(jnp.bfloat16)
    valid = neighbours >= 0
    safe_ids = jnp.where(valid, neighbours, 0).astype(jnp.int32)
    cnt = jnp.maximum(lax.optimization_barrier(jnp.sum(valid, axis=1)).astype(jnp.float32), 1.0)
    picked = embed[safe_ids].astype(jnp.float32) * valid[:, :, None].astype(jnp.float32)
    agg = (lax.optimization_barrier(jnp.sum(picked, axis=1)) / cnt[:, None]).astype(jnp.bfloat16)
    z = jnp.dot(embed, w_self, preferred_element_type=jnp.float32) + jnp.dot(agg, w_neigh, preferred_element_type=jnp.float32)
    mixed = jax.nn.gelu(z).astype(jnp.bfloat16)
    _, pullback = jax.vjp(jax.nn.gelu, z)
    dz = pullback(cotangent.astype(jnp.float32))[0].astype(jnp.bfloat16)
    d_agg = jnp.dot(dz, w_neigh.T, preferred_element_type=jnp.float32)
    msg = (d_agg / cnt[:, None]).astype(jnp.bfloat16)
    spread = jnp.broadcast_to(msg.astype(jnp.float32)[:, None, :], (NODES, FAN, D)) * valid[:, :, None].astype(jnp.float32)
    neighbour_sum = jnp.zeros((NODES, D), jnp.float32).at[safe_ids.reshape(-1)].add(spread.reshape(NODES * FAN, D))
    node_grad = (jnp.dot(dz, w_self.T, preferred_element_type=jnp.float32) + neighbour_sum).astype(jnp.bfloat16)
    factor = 1.0 / jnp.sqrt(jnp.float32(NODES))
    grad_w_self = jnp.dot(embed.T, dz, preferred_element_type=jnp.float32) * factor
    grad_w_neigh = jnp.dot(agg.T, dz, preferred_element_type=jnp.float32) * factor
    grad_w_out = jnp.dot(pooled.T, node_grad, preferred_element_type=jnp.float32) * factor
    return (mixed, node_grad, grad_w_self, grad_w_neigh, grad_w_out)
```

```python
import math

import jax
import jax.numpy as jnp
from jax import lax
from jax.experimental import pallas as pl
from jax.experimental.pallas import tpu as pltpu
from jax.sharding import PartitionSpec as P

MESH = pl.DeviceIdType.MESH
F32, BF16 = jnp.float32, jnp.bfloat16
HD = 64
NODE = 24
PAD = 32
DP, MP, NZ, NG, NY = 64, 4, 8, 8, 4
COLS, WIDTH = 256, 1024
SLOT = 16
EMPTY = 120.0
TEXTS = 2


def dot(a, b):
    return jnp.dot(a, b, preferred_element_type=F32)


def dot_nt(a, b):
    return lax.dot_general(a, b, (((1,), (1,)), ((), ())), preferred_element_type=F32)


def dot_tn(a, b):
    return lax.dot_general(a, b, (((0,), (0,)), ((), ())), preferred_element_type=F32)


def iota(shape, dim):
    return lax.broadcasted_iota(jnp.int32, shape, dim)


def pad_rows(x, rows):
    return jnp.concatenate([x, jnp.zeros((rows - x.shape[0], x.shape[1]), x.dtype)], axis=0)


def routing(nb_ref, want_ref, gh_ref, ght_ref, cnt_ref):
    nb = nb_ref[...]
    ids = nb.astype(F32)
    own = jnp.floor((ids + 0.5) * (1.0 / NODE))
    loc = ids - NODE * own
    live = nb >= 0
    cnt = jnp.maximum(jnp.sum(live.astype(F32), axis=1, keepdims=True), 1.0)
    cnt_ref[...] = jnp.concatenate(
        [jnp.broadcast_to(cnt, (NODE, COLS)), jnp.ones((PAD - NODE, COLS), F32)], axis=0
    )
    fan = nb.shape[1]
    groups = iota((NODE, DP), 1).astype(F32)
    hots = [(own[:, f : f + 1] == groups).astype(F32) for f in range(fan)]
    total = hots[0]
    for f in range(1, fan):
        total = total + hots[f]
    lower = (iota((NODE, NODE), 1) < iota((NODE, NODE), 0)).astype(BF16)
    run = dot(lower, total.astype(BF16))
    spots = iota((NODE, DP * SLOT), 1).astype(F32)
    left = jnp.zeros((NODE, DP * SLOT), F32)
    right = jnp.zeros((NODE, DP * SLOT), F32)
    names = jnp.zeros((NODE, DP * SLOT), F32)
    for f in range(fan):
        rank = jnp.sum(hots[f] * run, axis=1, keepdims=True)
        run = run + hots[f]
        at = jnp.where(live[:, f : f + 1], own[:, f : f + 1] * SLOT + rank, -1000.0)
        name = loc[:, f : f + 1]
        is_left = spots == at
        is_right = spots == at + 8.0
        left = left + is_left.astype(F32)
        right = right + is_right.astype(F32)
        names = names + jnp.where(is_left, name - EMPTY, 0.0)
        names = names + jnp.where(is_right, name + (PAD - EMPTY), 0.0)
    gap = jnp.zeros((PAD - NODE, DP * SLOT), F32)
    both = jnp.concatenate([left, gap, right, gap], axis=0)
    gh_ref[...] = both.astype(BF16)
    ght_ref[...] = jnp.transpose(pad_rows(both, 128)).astype(BF16)
    spread = jnp.transpose(pad_rows(names, 128)).astype(BF16)
    want_ref[...] = (dot(spread, jnp.ones((128, 128), BF16)) + EMPTY).astype(BF16)


def attention_kernel(tx_ref, w_ref, nb_ref, pooled_ref, tmean_ref, want_ref, gh_ref, ght_ref, cnt_ref, wp, acc, tacc):
    step = pl.program_id(0)
    low = iota((1, 128), 1) < HD

    @pl.when(step == 0)
    def _():
        for pair in range(2):
            base = pair * 384
            a = w_ref[:, base : base + 128].astype(F32)
            b = w_ref[:, base + 128 : base + 256].astype(F32)
            c = w_ref[:, base + 256 : base + 384].astype(F32)
            wp[:, pair * 128 : pair * 128 + 128] = jnp.where(low, a, b).astype(BF16)
            wp[:, 256 + pair * 128 : 384 + pair * 128] = pltpu.roll(jnp.where(low, c, a), HD, 1).astype(BF16)
            wp[:, 512 + pair * 128 : 640 + pair * 128] = jnp.where(low, b, c).astype(BF16)
        routing(nb_ref, want_ref, gh_ref, ght_ref, cnt_ref)

    rows = TEXTS * 128
    x = tx_ref[...].reshape(rows, WIDTH)
    q = dot(x, wp[:, 0:256]).astype(BF16)
    k = dot(x, wp[:, 256:512]).astype(BF16)
    v = dot(x, wp[:, 512:768]).astype(BF16).astype(F32)
    ones = ((iota((256, 128), 0) < 128) == (iota((256, 128), 1) < HD)).astype(BF16)
    scale = 1.0 / (math.sqrt(HD) * math.log(2.0))
    zero = jnp.zeros((), BF16)
    for t in range(TEXTS):
        parts = []
        for pair in range(2):
            cols = slice(pair * 128, pair * 128 + 128)
            qt = q[t * 128 : t * 128 + 128, cols]
            kt = k[t * 128 : t * 128 + 128, cols]
            vt = v[t * 128 : t * 128 + 128, cols]
            two = jnp.concatenate([jnp.where(low, qt, zero), jnp.where(low, zero, qt)], axis=0)
            s = dot_nt(kt, two)
            e = jnp.exp2((s - jnp.max(s, axis=0, keepdims=True)) * scale)
            p = (e / jnp.sum(e, axis=0, keepdims=True)).astype(BF16)
            parts.append(jnp.sum(dot(p, ones) * vt, axis=0, keepdims=True) * (1.0 / 128))
        row = jnp.concatenate(parts, axis=1)
        acc[pl.ds(step * TEXTS + t, 1), :] = row
        mine = tx_ref[t, :, pl.ds(pl.multiple_of(lax.axis_index("mp") * COLS, COLS), COLS)]
        tacc[pl.ds(step * TEXTS + t, 1), :] = jnp.sum(mine.astype(F32), axis=0, keepdims=True) * (1.0 / 128)

    @pl.when(step == pl.num_programs(0) - 1)
    def _():
        pooled_ref[...] = pad_rows(acc[...], PAD).astype(BF16)
        tmean_ref[...] = tacc[...]


def attention(texts, w_qkv, neighbours):
    steps = NODE // TEXTS
    whole = lambda *shape: pl.BlockSpec(shape, lambda i: (0,) * len(shape))
    return pl.pallas_call(
        attention_kernel,
        grid=(steps,),
        out_shape=[
            jax.ShapeDtypeStruct((PAD, COLS), BF16),
            jax.ShapeDtypeStruct((NODE, COLS), F32),
            jax.ShapeDtypeStruct((DP * SLOT, 128), BF16),
            jax.ShapeDtypeStruct((2 * PAD, DP * SLOT), BF16),
            jax.ShapeDtypeStruct((DP * SLOT, 128), BF16),
            jax.ShapeDtypeStruct((PAD, COLS), F32),
        ],
        in_specs=[
            pl.BlockSpec((TEXTS, 128, WIDTH), lambda i: (i, 0, 0)),
            whole(WIDTH, 768),
            whole(NODE, 16),
        ],
        out_specs=[
            whole(PAD, COLS),
            whole(NODE, COLS),
            whole(DP * SLOT, 128),
            whole(2 * PAD, DP * SLOT),
            whole(DP * SLOT, 128),
            whole(PAD, COLS),
        ],
        scratch_shapes=[
            pltpu.VMEM((WIDTH, 768), BF16),
            pltpu.VMEM((NODE, COLS), F32),
            pltpu.VMEM((NODE, COLS), F32),
        ],
        compiler_params=pltpu.CompilerParams(
            dimension_semantics=("arbitrary",), vmem_limit_bytes=40 * 2**20
        ),
        cost_estimate=pl.CostEstimate(flops=6 * 10**9, bytes_accessed=9 * 10**6, transcendentals=1600000),
    )(texts, w_qkv, neighbours)


ASK, POOL_SUM, ROWS, EMB_G, POOL_G, AGG_G, Z_SUM, DZ, DZ_G, BACK, NG_G, SN_RS, SN_AG, OUT_RS, OUT_AG = range(15)


def graph_kernel(
    pooled, tmean, want, gh, ght, cnt, w_out, w_self, w_neigh, cot,
    mixed, ngrad, o_self, o_neigh, o_out,
    asked, sbuf, rbuf, sbuf2, rbuf2, sel_t, part, sums, zpart, zsums, e2, m2,
    emb_g, pool_g, agg_g, dzf, dz2, dz_g, ng2, ng_g, sn_s, sn_r, fin_sn, out_s, out_r, fin_out,
    ssem, rsem, y_s, y_r, c_s, c_r,
):
    m, d = lax.axis_index("mp"), lax.axis_index("dp")
    z, g = d // NG, d % NG
    y, c = g // 2, g % 2
    is_diag = (g // 2) == m

    def send(src, dst, phase, dp, mp):
        pltpu.make_async_remote_copy(
            src_ref=src, dst_ref=dst, send_sem=ssem.at[phase], recv_sem=rsem.at[phase],
            device_id=(dp, mp), device_id_type=MESH,
        ).start()

    def got(ref, phase):
        pltpu.make_async_copy(ref, ref, rsem.at[phase]).wait()

    def sent(ref, phase):
        pltpu.make_async_copy(ref, ref, ssem.at[phase]).wait()

    def over(count, body):
        def step(i, carry):
            body(i)
            return carry

        lax.fori_loop(1, count, step, 0)

    def to_dp(src, dst, phase):
        def one(i):
            to = (d + i) % DP
            send(src.at[to], dst.at[d], phase, to, m)

        over(DP, one)
        dst[d] = src[d]

    def to_mp(src, dst, phase):
        for i in range(1, MP):
            to = (m + i) % MP
            send(src.at[to], dst.at[m], phase, d, to)
        dst[m] = src[m]

    def to_group(block, phase):
        for i in range(1, NG):
            send(block.at[g], block.at[g], phase, z * NG + (g + i) % NG, m)

    def to_columns(src, dst, phase):
        def one(i, carry):
            mp, half = i // 2, i % 2
            at = 2 * m + half
            here = jnp.logical_and(mp == m, at == g)

            @pl.when(jnp.logical_not(here))
            def _():
                send(src.at[half], dst.at[g], phase, z * NG + at, mp)

            @pl.when(here)
            def _():
                dst[g] = src[half]

            return carry

        lax.fori_loop(0, 2 * MP, one, 0)

    def got_columns(dst, phase):
        @pl.when(is_diag)
        def _():
            got(dst.at[pl.ds(0, NG - 1)], phase)

        @pl.when(jnp.logical_not(is_diag))
        def _():
            got(dst, phase)

    def sent_columns(dst, phase):
        @pl.when(is_diag)
        def _():
            sent(dst.at[pl.ds(0, NG - 1)], phase)

        @pl.when(jnp.logical_not(is_diag))
        def _():
            sent(dst, phase)

    def scatter_z(src, dst, phase):
        for i in range(1, NZ):
            to = (z + i) % NZ
            send(src.at[to], dst.at[z], phase, to * NG + g, m)
        dst[z] = src[z]

    def gather_z(fin, phase):
        for i in range(1, NZ):
            to = (z + i) % NZ
            send(fin.at[g, z], fin.at[g, z], phase, to * NG + g, m)

    def y_copy(fin, at, to, k):
        return pltpu.make_async_remote_copy(
            src_ref=fin.at[at], dst_ref=fin.at[at], send_sem=y_s.at[k], recv_sem=y_r.at[k],
            device_id=(z * NG + to * 2 + c, m), device_id_type=MESH,
        )

    def c_copy(fin, at, k):
        return pltpu.make_async_remote_copy(
            src_ref=fin.at[at], dst_ref=fin.at[at], send_sem=c_s.at[k], recv_sem=c_r.at[k],
            device_id=(z * NG + y * 2 + 1 - c, m), device_id_type=MESH,
        )

    bar = pltpu.get_barrier_semaphore()
    over(DP, lambda i: pl.semaphore_signal(bar, inc=1, device_id=((d + i) % DP, m), device_id_type=MESH))
    for i in range(1, MP):
        pl.semaphore_signal(bar, inc=1, device_id=(d, (m + i) % MP), device_id_type=MESH)

    def greet(i, carry):
        @pl.when(jnp.logical_not(jnp.logical_and(is_diag, i == g)))
        def _():
            pl.semaphore_signal(bar, inc=1, device_id=(z * NG + i, g // 2), device_id_type=MESH)

        return carry

    lax.fori_loop(0, NG, greet, 0)

    first = dot(pooled[...], w_out[...])
    for j in range(MP):
        part[j] = first[:NODE, j * COLS : (j + 1) * COLS]
    e2[...] = jnp.zeros_like(e2)
    m2[...] = jnp.zeros_like(m2)
    pool_g[g] = pooled[...]

    pl.semaphore_wait(bar, DP - 1 + MP - 1 + 2 * MP - is_diag.astype(jnp.int32))

    to_mp(part, sums, POOL_SUM)
    to_dp(want, asked, ASK)
    got(sums.at[pl.ds(0, MP - 1)], POOL_SUM)
    embed = tmean[...] + (sums[0] + sums[1] + sums[2] + sums[3])
    embed = pad_rows(embed, PAD).astype(BF16)
    e2[0:PAD, :] = embed[:, :128]
    e2[PAD : 2 * PAD, :] = embed[:, 128:]
    emb_g[g] = embed

    got(asked.at[pl.ds(0, DP - 1)], ASK)
    names = asked[...].reshape(DP * SLOT, 128).astype(F32)
    sel = (names == iota((DP * SLOT, 128), 1).astype(F32)).astype(F32)
    sbuf[...] = dot(sel.astype(BF16), e2[...]).astype(BF16).reshape(DP, SLOT, 128)
    to_dp(sbuf, rbuf, ROWS)
    to_group(emb_g, EMB_G)
    to_group(pool_g, POOL_G)
    sel_t[...] = jnp.transpose(sel)[: 2 * PAD].astype(BF16)
    zself = dot(embed, w_self[...])
    got(rbuf.at[pl.ds(0, DP - 1)], ROWS)
    two = dot(gh[...], rbuf[...].reshape(DP * SLOT, 128))
    agg = (jnp.concatenate([two[:PAD], two[PAD:]], axis=1) / cnt[...]).astype(BF16)
    zfull = zself + dot(agg, w_neigh[...])
    for j in range(MP):
        zpart[j] = zfull[:NODE, j * COLS : (j + 1) * COLS]
    to_mp(zpart, zsums, Z_SUM)
    agg_g[g] = agg
    to_group(agg_g, AGG_G)
    got(zsums.at[pl.ds(0, MP - 1)], Z_SUM)
    zc = zsums[0] + zsums[1] + zsums[2] + zsums[3]

    root = math.sqrt(2.0 / math.pi)
    th = jnp.tanh(root * (zc + 0.044715 * (zc * zc * zc)))
    cdf = 0.5 * (1.0 + th)
    slope = cdf + zc * (0.5 * (1.0 - th * th) * (root * (1.0 + (3 * 0.044715) * (zc * zc))))
    dz = pad_rows(cot[...].astype(F32) * slope, PAD).astype(BF16)
    dzf[m] = dz
    for i in range(1, MP):
        send(dzf.at[m], dzf.at[m], DZ, d, (m + i) % MP)
    dz2[0] = dz[:, :128]
    dz2[1] = dz[:, 128:]
    to_columns(dz2, dz_g, DZ_G)
    mixed[...] = (zc * cdf).astype(BF16)
    got(dzf.at[pl.ds(0, MP - 1)], DZ)

    dagg = dot_nt(dzf[0], w_neigh[:, 0:COLS])
    for j in range(1, MP):
        dagg = dagg + dot_nt(dzf[j], w_neigh[:, j * COLS : (j + 1) * COLS])
    msg = (dagg / cnt[...]).astype(BF16)
    m2[0:PAD, :] = msg[:, :128]
    m2[PAD : 2 * PAD, :] = msg[:, 128:]
    sbuf2[...] = dot(ght[...], m2[...]).astype(BF16).reshape(DP, SLOT, 128)
    to_dp(sbuf2, rbuf2, BACK)
    own = dot_nt(dzf[0], w_self[:, 0:COLS])
    for j in range(1, MP):
        own = own + dot_nt(dzf[j], w_self[:, j * COLS : (j + 1) * COLS])

    got_columns(dz_g, DZ_G)
    got(emb_g.at[pl.ds(0, NG - 1)], EMB_G)
    got(agg_g.at[pl.ds(0, NG - 1)], AGG_G)
    rhs = dz_g[...].reshape(NG * PAD, 128)
    sn_s[:, 0] = dot_tn(emb_g[...].reshape(NG * PAD, COLS), rhs).astype(BF16).reshape(NZ, PAD, 128)
    sn_s[:, 1] = dot_tn(agg_g[...].reshape(NG * PAD, COLS), rhs).astype(BF16).reshape(NZ, PAD, 128)
    scatter_z(sn_s, sn_r, SN_RS)

    got(rbuf2.at[pl.ds(0, DP - 1)], BACK)
    two = dot(sel_t[...], rbuf2[...].reshape(DP * SLOT, 128))
    grad = (own + jnp.concatenate([two[:PAD], two[PAD:]], axis=1)).astype(BF16)
    ng2[0] = grad[:, :128]
    ng2[1] = grad[:, 128:]
    to_columns(ng2, ng_g, NG_G)
    ngrad[...] = grad[:NODE]

    factor = 1.0 / math.sqrt(NODE * DP)

    def z_total(buf):
        total = buf[0].astype(F32)
        for i in range(1, NZ):
            total = total + buf[i].astype(F32)
        return (total * factor).astype(BF16)

    got(sn_r.at[pl.ds(0, NZ - 1)], SN_RS)
    fin_sn[g, z] = z_total(sn_r)
    gather_z(fin_sn, SN_AG)

    got(pool_g.at[pl.ds(0, NG - 1)], POOL_G)
    got_columns(ng_g, NG_G)
    out = dot_tn(pool_g[...].reshape(NG * PAD, COLS), ng_g[...].reshape(NG * PAD, 128))
    out_s[...] = out.astype(BF16).reshape(NZ, PAD, 128)
    scatter_z(out_s, out_r, OUT_RS)

    got(fin_sn.at[0, pl.ds(0, NZ - 1)], SN_AG)
    for i in range(1, NY):
        y_copy(fin_sn, g, (y + i) % NY, i - 1).start()
    c_copy(fin_sn, g, 0).start()

    got(out_r.at[pl.ds(0, NZ - 1)], OUT_RS)
    fin_out[g, z] = z_total(out_r)
    gather_z(fin_out, OUT_AG)

    def forward(fin, first):
        for i in range(1, NY):
            at = ((y + NY - i) % NY) * 2 + c
            y_copy(fin, at, y, first + i - 1).wait_recv()
            c_copy(fin, at, (first // 3) * 4 + i).start()

    forward(fin_sn, 0)
    got(fin_out.at[0, pl.ds(0, NZ - 1)], OUT_AG)
    for i in range(1, NY):
        y_copy(fin_out, g, (y + i) % NY, 3 + i - 1).start()
    c_copy(fin_out, g, 4).start()

    for i in range(NY):
        c_copy(fin_sn, ((y + NY - i) % NY) * 2 + 1 - c, i).wait_recv()
    for j in range(NG):
        cols = slice(j * 128, j * 128 + 128)
        o_self[:, cols] = fin_sn[j, :, 0].reshape(COLS, 128).astype(F32)
        o_neigh[:, cols] = fin_sn[j, :, 1].reshape(COLS, 128).astype(F32)

    forward(fin_out, 3)
    for i in range(NY):
        c_copy(fin_out, ((y + NY - i) % NY) * 2 + 1 - c, 4 + i).wait_recv()
    for j in range(NG):
        o_out[:, j * 128 : j * 128 + 128] = fin_out[j].reshape(COLS, 128).astype(F32)

    sent(sums.at[pl.ds(0, MP - 1)], POOL_SUM)
    sent(asked.at[pl.ds(0, DP - 1)], ASK)
    sent(rbuf.at[pl.ds(0, DP - 1)], ROWS)
    sent(emb_g.at[pl.ds(0, NG - 1)], EMB_G)
    sent(pool_g.at[pl.ds(0, NG - 1)], POOL_G)
    sent(agg_g.at[pl.ds(0, NG - 1)], AGG_G)
    sent(zsums.at[pl.ds(0, MP - 1)], Z_SUM)
    sent(dzf.at[pl.ds(0, MP - 1)], DZ)
    sent_columns(dz_g, DZ_G)
    sent(rbuf2.at[pl.ds(0, DP - 1)], BACK)
    sent_columns(ng_g, NG_G)
    sent(sn_r.at[pl.ds(0, NZ - 1)], SN_RS)
    sent(fin_sn.at[0, pl.ds(0, NZ - 1)], SN_AG)
    sent(out_r.at[pl.ds(0, NZ - 1)], OUT_RS)
    sent(fin_out.at[0, pl.ds(0, NZ - 1)], OUT_AG)
    for k in range(3):
        y_copy(fin_sn, g, y, k).wait_send()
        y_copy(fin_out, g, y, 3 + k).wait_send()
    for k in range(NY):
        c_copy(fin_sn, g, k).wait_send()
        c_copy(fin_out, g, 4 + k).wait_send()


def graph(pooled, tmean, want, gh, ght, cnt, w_out, w_self, w_neigh, cot):
    vmem = pl.BlockSpec(memory_space=pltpu.VMEM)
    return pl.pallas_call(
        graph_kernel,
        out_shape=[
            jax.ShapeDtypeStruct((NODE, COLS), BF16),
            jax.ShapeDtypeStruct((NODE, COLS), BF16),
            jax.ShapeDtypeStruct((COLS, WIDTH), F32),
            jax.ShapeDtypeStruct((COLS, WIDTH), F32),
            jax.ShapeDtypeStruct((COLS, WIDTH), F32),
        ],
        in_specs=[vmem] * 10,
        out_specs=[vmem] * 5,
        scratch_shapes=[
            pltpu.VMEM((DP, SLOT, 128), BF16),
            pltpu.VMEM((DP, SLOT, 128), BF16),
            pltpu.VMEM((DP, SLOT, 128), BF16),
            pltpu.VMEM((DP, SLOT, 128), BF16),
            pltpu.VMEM((DP, SLOT, 128), BF16),
            pltpu.VMEM((2 * PAD, DP * SLOT), BF16),
            pltpu.VMEM((MP, NODE, COLS), F32),
            pltpu.VMEM((MP, NODE, COLS), F32),
            pltpu.VMEM((MP, NODE, COLS), F32),
            pltpu.VMEM((MP, NODE, COLS), F32),
            pltpu.VMEM((128, 128), BF16),
            pltpu.VMEM((128, 128), BF16),
            pltpu.VMEM((NG, PAD, COLS), BF16),
            pltpu.VMEM((NG, PAD, COLS), BF16),
            pltpu.VMEM((NG, PAD, COLS), BF16),
            pltpu.VMEM((MP, PAD, COLS), BF16),
            pltpu.VMEM((2, PAD, 128), BF16),
            pltpu.VMEM((NG, PAD, 128), BF16),
            pltpu.VMEM((2, PAD, 128), BF16),
            pltpu.VMEM((NG, PAD, 128), BF16),
            pltpu.VMEM((NZ, 2, PAD, 128), BF16),
            pltpu.VMEM((NZ, 2, PAD, 128), BF16),
            pltpu.VMEM((NG, NZ, 2, PAD, 128), BF16),
            pltpu.VMEM((NZ, PAD, 128), BF16),
            pltpu.VMEM((NZ, PAD, 128), BF16),
            pltpu.VMEM((NG, NZ, PAD, 128), BF16),
            pltpu.SemaphoreType.DMA((15,)),
            pltpu.SemaphoreType.DMA((15,)),
            pltpu.SemaphoreType.DMA((6,)),
            pltpu.SemaphoreType.DMA((6,)),
            pltpu.SemaphoreType.DMA((8,)),
            pltpu.SemaphoreType.DMA((8,)),
        ],
        compiler_params=pltpu.CompilerParams(
            collective_id=0, has_side_effects=True, vmem_limit_bytes=40 * 2**20
        ),
        cost_estimate=pl.CostEstimate(flops=10**9, bytes_accessed=8 * 10**6, transcendentals=10**4),
    )(pooled, tmean, want.reshape(DP, SLOT, 128), gh, ght, cnt, w_out, w_self, w_neigh, cot)


def per_device(texts, w_qkv, w_out, w_self, w_neigh, neighbours, cotangent):
    pooled, tmean, want, gh, ght, cnt = attention(texts, w_qkv, neighbours)
    return tuple(graph(pooled, tmean, want, gh, ght, cnt, w_out, w_self, w_neigh, cotangent))


def solution(mesh):
    return jax.shard_map(
        per_device,
        mesh=mesh,
        in_specs=(
            P("dp", None, None),
            P(None, "mp"),
            P("mp", None),
            P("mp", None),
            P("mp", None),
            P("dp", None),
            P("dp", "mp"),
        ),
        out_specs=(P("dp", "mp"), P("dp", "mp"), P("mp", None), P("mp", None), P("mp", None)),
        check_vma=False,
    )
```

```python
import math

import jax
import jax.numpy as jnp
from jax import lax
from jax.experimental import pallas as pl
from jax.experimental.pallas import tpu as pltpu
from jax.sharding import PartitionSpec as P

MESH = pl.DeviceIdType.MESH
F32, BF16 = jnp.float32, jnp.bfloat16
HD = 64
NODE = 24
PAD = 32
DP, MP, NZ, NG, NY = 64, 4, 8, 8, 4
COLS, WIDTH = 256, 1024
SLOT = 16
EMPTY = 120.0
VMEM_LIMIT = 60 * 2**20
TEXTS = 8


def dot(a, b):
    return jnp.dot(a, b, preferred_element_type=F32)


def dot_nt(a, b):
    return lax.dot_general(a, b, (((1,), (1,)), ((), ())), preferred_element_type=F32)


def dot_tn(a, b):
    return lax.dot_general(a, b, (((0,), (0,)), ((), ())), preferred_element_type=F32)


def iota(shape, dim):
    return lax.broadcasted_iota(jnp.int32, shape, dim)


def pad_rows(x, rows):
    return jnp.concatenate([x, jnp.zeros((rows - x.shape[0], x.shape[1]), x.dtype)], axis=0)


def routing(ids_ref, want, gh, ght, cnt_out):
    ids = jnp.transpose(ids_ref[...].astype(F32))
    own = jnp.floor((ids + 0.5) * (1.0 / NODE))
    loc = ids - NODE * own
    live = ids >= 0.0
    cnt = jnp.maximum(jnp.sum(live.astype(F32), axis=1, keepdims=True), 1.0)
    cnt_out[...] = jnp.concatenate(
        [jnp.broadcast_to(cnt, (NODE, COLS)), jnp.ones((PAD - NODE, COLS), F32)], axis=0
    )
    fan = ids.shape[1]
    groups = iota((NODE, DP), 1).astype(F32)
    hots = [(own[:, f : f + 1] == groups).astype(F32) for f in range(fan)]
    total = hots[0]
    for f in range(1, fan):
        total = total + hots[f]
    lower = (iota((NODE, NODE), 1) < iota((NODE, NODE), 0)).astype(BF16)
    run = dot(lower, total.astype(BF16))
    spots = iota((NODE, DP * SLOT), 1).astype(F32)
    left = jnp.zeros((NODE, DP * SLOT), F32)
    right = jnp.zeros((NODE, DP * SLOT), F32)
    names = jnp.zeros((NODE, DP * SLOT), F32)
    for f in range(fan):
        rank = jnp.sum(hots[f] * run, axis=1, keepdims=True)
        run = run + hots[f]
        at = jnp.where(live[:, f : f + 1], own[:, f : f + 1] * SLOT + rank, -1000.0)
        name = loc[:, f : f + 1]
        is_left = spots == at
        is_right = spots == at + 8.0
        left = left + is_left.astype(F32)
        right = right + is_right.astype(F32)
        names = names + jnp.where(is_left, name - EMPTY, 0.0)
        names = names + jnp.where(is_right, name + (PAD - EMPTY), 0.0)
    gap = jnp.zeros((PAD - NODE, DP * SLOT), F32)
    both = jnp.concatenate([left, gap, right, gap], axis=0)
    gh[...] = both.astype(BF16)
    ght[...] = jnp.transpose(pad_rows(both, 128)).astype(BF16)
    spread = jnp.transpose(pad_rows(names, 128)).astype(BF16)
    want[...] = (dot(spread, jnp.ones((128, 128), BF16)) + EMPTY).astype(BF16).reshape(DP, SLOT, 128)


def order_columns(w, wp):
    low = iota((1, 128), 1) < HD
    for pair in range(2):
        base = pair * 384
        at = pair * 128
        a = w[:, base : base + 128].astype(F32)
        b = w[:, base + 128 : base + 256].astype(F32)
        c = w[:, base + 256 : base + 384].astype(F32)
        wp[:, at : at + 128] = jnp.where(low, a, b).astype(BF16)
        wp[:, 256 + at : 384 + at] = pltpu.roll(jnp.where(low, c, a), HD, 1).astype(BF16)
        wp[:, 512 + at : 640 + at] = jnp.where(low, b, c).astype(BF16)


def attend(qkv):
    low = iota((1, 128), 1) < HD
    scale = 1.0 / (math.sqrt(HD) * math.log(2.0))
    zero = jnp.zeros((), BF16)
    texts = []
    for t in range(TEXTS):
        rows = slice(t * 128, t * 128 + 128)
        parts = []
        for pair in range(2):
            at = pair * 128
            qt = qkv[rows, at : at + 128]
            kt = qkv[rows, 256 + at : 384 + at]
            vt = qkv[rows, 512 + at : 640 + at].astype(F32)
            two = jnp.concatenate([jnp.where(low, qt, zero), jnp.where(low, zero, qt)], axis=0)
            s = dot_nt(kt, two)
            e = jnp.exp2((s - jnp.max(s, axis=0, keepdims=True)) * scale)
            p = (e * (1.0 / jnp.sum(e, axis=0, keepdims=True))).astype(BF16).astype(F32)
            first = jnp.sum(p[:, :128], axis=1, keepdims=True)
            second = jnp.sum(p[:, 128:], axis=1, keepdims=True)
            parts.append(jnp.sum(jnp.where(low, first, second) * vt, axis=0, keepdims=True))
        texts.append(jnp.concatenate(parts, axis=1))
    return jnp.concatenate(texts, axis=0) * (1.0 / 128)


ASK, POOL_SUM, ROWS, EMB_G, POOL_G, AGG_G, Z_SUM, DZ, DZ_G, BACK, NG_G, SN_RS, SN_AG, OUT_RS, OUT_AG = range(15)


def step_kernel(
    texts_in, qkv_in, out_in, self_in, neigh_in, ids_in, cot_in,
    o_mixed, o_ngrad, o_sn, o_out,
    mixed, ngrad, fin_sn, fin_out, tx, wq, wp, qkv, w_out, w_self, w_neigh, ids, cot, acc, tmean, pooled, want, gh, ght, cnt,
    asked, sbuf, rbuf, sbuf2, rbuf2, sel_t, part, sums, zpart, zsums, e2, m2,
    emb_g, pool_g, agg_g, dzf, dz2, dz_g, ng2, ng_g, sn_s, sn_r, out_s, out_r,
    tsem, lsem, osem, ssem, rsem, y_s, y_r, c_s, c_r,
):
    m, d = lax.axis_index("mp"), lax.axis_index("dp")
    z, g = d // NG, d % NG
    y, c = g // 2, g % 2
    is_diag = (g // 2) == m

    def send(src, dst, phase, dp, mp):
        pltpu.make_async_remote_copy(
            src_ref=src, dst_ref=dst, send_sem=ssem.at[phase], recv_sem=rsem.at[phase],
            device_id=(dp, mp), device_id_type=MESH,
        ).start()

    def got(ref, phase):
        pltpu.make_async_copy(ref, ref, rsem.at[phase]).wait()

    def sent(ref, phase):
        pltpu.make_async_copy(ref, ref, ssem.at[phase]).wait()

    pending = []

    def emit(k, src, dst):
        copy = pltpu.make_async_copy(src, dst, osem.at[k])
        copy.start()
        pending.append(copy.wait)

    def later(ref, phase):
        pending.append(lambda: sent(ref, phase))

    def over(count, body):
        def step(i, carry):
            body(i)
            return carry

        lax.fori_loop(1, count, step, 0)

    def to_dp(src, dst, phase):
        for k in (4, 3, 5, 2, 6, 1, 7, 0):

            def one(i, carry):
                to = ((z + k) % NZ) * NG + (g + i) % NG
                send(src.at[to], dst.at[d], phase, to, m)
                return carry

            lax.fori_loop(1 if k == 0 else 0, NG, one, 0)
        dst[d] = src[d]
        later(dst.at[pl.ds(0, DP - 1)], phase)

    def to_mp(src, dst, phase):
        for i in range(1, MP):
            to = (m + i) % MP
            send(src.at[to], dst.at[m], phase, d, to)
        dst[m] = src[m]
        later(dst.at[pl.ds(0, MP - 1)], phase)

    def to_group(block, phase):
        for i in range(1, NG):
            send(block.at[g], block.at[g], phase, z * NG + (g + i) % NG, m)
        later(block.at[pl.ds(0, NG - 1)], phase)

    def to_columns(src, dst, phase):
        def one(i, carry):
            mp, half = i // 2, i % 2
            at = 2 * m + half
            here = jnp.logical_and(mp == m, at == g)

            @pl.when(jnp.logical_not(here))
            def _():
                send(src.at[half], dst.at[g], phase, z * NG + at, mp)

            @pl.when(here)
            def _():
                dst[g] = src[half]

            return carry

        lax.fori_loop(0, 2 * MP, one, 0)
        pending.append(lambda: sent_columns(dst, phase))

    def got_columns(dst, phase):
        @pl.when(is_diag)
        def _():
            got(dst.at[pl.ds(0, NG - 1)], phase)

        @pl.when(jnp.logical_not(is_diag))
        def _():
            got(dst, phase)

    def sent_columns(dst, phase):
        @pl.when(is_diag)
        def _():
            sent(dst.at[pl.ds(0, NG - 1)], phase)

        @pl.when(jnp.logical_not(is_diag))
        def _():
            sent(dst, phase)

    def scatter_z(src, dst, phase):
        for i in range(1, NZ):
            to = (z + i) % NZ
            send(src.at[to], dst.at[z], phase, to * NG + g, m)
        dst[z] = src[z]
        later(dst.at[pl.ds(0, NZ - 1)], phase)

    def gather_z(fin, phase):
        for i in range(1, NZ):
            to = (z + i) % NZ
            send(fin.at[g, z], fin.at[g, z], phase, to * NG + g, m)
        later(fin.at[0, pl.ds(0, NZ - 1)], phase)

    def y_copy(fin, at, to, k):
        return pltpu.make_async_remote_copy(
            src_ref=fin.at[at], dst_ref=fin.at[at], send_sem=y_s.at[k], recv_sem=y_r.at[k],
            device_id=(z * NG + to * 2 + c, m), device_id_type=MESH,
        )

    def c_copy(fin, at, k):
        return pltpu.make_async_remote_copy(
            src_ref=fin.at[at], dst_ref=fin.at[at], send_sem=c_s.at[k], recv_sem=c_r.at[k],
            device_id=(z * NG + y * 2 + 1 - c, m), device_id_type=MESH,
        )

    def y_sends(fin, first):
        for i in range(1, NY):
            copy = y_copy(fin, g, (y + i) % NY, first + i - 1)
            copy.start()
            pending.append(copy.wait_send)
        own = c_copy(fin, g, (first // 3) * 4)
        own.start()
        pending.append(own.wait_send)

    weight = pltpu.make_async_copy(qkv_in, wq, lsem.at[0])
    names_in = pltpu.make_async_copy(ids_in, ids, lsem.at[1])
    names_in.start()
    weight.start()
    chunks = NODE // TEXTS

    def chunk(i):
        rows = pl.ds(i * TEXTS, TEXTS)
        return pltpu.make_async_copy(texts_in.at[rows], tx.at[rows], tsem.at[i])

    for i in range(chunks):
        chunk(i).start()
    others = [
        pltpu.make_async_copy(src, dst, lsem.at[2 + i])
        for i, (src, dst) in enumerate(
            [(out_in, w_out), (self_in, w_self), (neigh_in, w_neigh), (cot_in, cot)]
        )
    ]
    for copy in others:
        copy.start()

    bar = pltpu.get_barrier_semaphore()
    over(DP, lambda i: pl.semaphore_signal(bar, inc=1, device_id=((d + i) % DP, m), device_id_type=MESH))
    for i in range(1, MP):
        pl.semaphore_signal(bar, inc=1, device_id=(d, (m + i) % MP), device_id_type=MESH)

    def greet(i, carry):
        @pl.when(jnp.logical_not(jnp.logical_and(is_diag, i == g)))
        def _():
            pl.semaphore_signal(bar, inc=1, device_id=(z * NG + i, g // 2), device_id_type=MESH)

        return carry

    lax.fori_loop(0, NG, greet, 0)

    names_in.wait()
    routing(ids, want, gh, ght, cnt)
    e2[...] = jnp.zeros_like(e2)
    m2[...] = jnp.zeros_like(m2)
    weight.wait()
    order_columns(wq, wp)
    pl.semaphore_wait(bar, DP - 1 + MP - 1 + 2 * MP - is_diag.astype(jnp.int32))
    to_dp(want, asked, ASK)

    def work(i, carry):
        chunk(i).wait()
        rows = pl.ds(pl.multiple_of(i * TEXTS, TEXTS), TEXTS)
        qkv[...] = dot(tx[rows].reshape(TEXTS * 128, WIDTH), wp[...]).astype(BF16)
        acc[rows, :] = attend(qkv)
        mine = tx[rows, :, pl.ds(pl.multiple_of(m * COLS, COLS), COLS)]
        tmean[rows, :] = jnp.sum(mine.astype(F32), axis=1) * (1.0 / 128)
        return carry

    lax.fori_loop(0, chunks, work, 0)
    for copy in others:
        copy.wait()
    pooled[...] = pad_rows(acc[...], PAD).astype(BF16)
    pool_g[g] = pooled[...]
    first = dot(pooled[...], w_out[...])
    for j in range(MP):
        part[j] = first[:NODE, j * COLS : (j + 1) * COLS]

    to_mp(part, sums, POOL_SUM)
    got(sums.at[pl.ds(0, MP - 1)], POOL_SUM)
    embed = tmean[...] + (sums[0] + sums[1] + sums[2] + sums[3])
    embed = pad_rows(embed, PAD).astype(BF16)
    e2[0:PAD, :] = embed[:, :128]
    e2[PAD : 2 * PAD, :] = embed[:, 128:]
    emb_g[g] = embed

    got(asked.at[pl.ds(0, DP - 1)], ASK)
    names = asked[...].reshape(DP * SLOT, 128).astype(F32)
    sel = (names == iota((DP * SLOT, 128), 1).astype(F32)).astype(F32)
    sbuf[...] = dot(sel.astype(BF16), e2[...]).astype(BF16).reshape(DP, SLOT, 128)
    to_dp(sbuf, rbuf, ROWS)
    to_group(emb_g, EMB_G)
    to_group(pool_g, POOL_G)
    sel_t[...] = jnp.transpose(sel)[: 2 * PAD].astype(BF16)
    zself = dot(embed, w_self[...])
    got(rbuf.at[pl.ds(0, DP - 1)], ROWS)
    two = dot(gh[...], rbuf[...].reshape(DP * SLOT, 128))
    agg = (jnp.concatenate([two[:PAD], two[PAD:]], axis=1) / cnt[...]).astype(BF16)
    zfull = zself + dot(agg, w_neigh[...])
    for j in range(MP):
        zpart[j] = zfull[:NODE, j * COLS : (j + 1) * COLS]
    to_mp(zpart, zsums, Z_SUM)
    agg_g[g] = agg
    to_group(agg_g, AGG_G)
    got(zsums.at[pl.ds(0, MP - 1)], Z_SUM)
    zc = zsums[0] + zsums[1] + zsums[2] + zsums[3]

    root = math.sqrt(2.0 / math.pi)
    th = jnp.tanh(root * (zc + 0.044715 * (zc * zc * zc)))
    cdf = 0.5 * (1.0 + th)
    slope = cdf + zc * (0.5 * (1.0 - th * th) * (root * (1.0 + (3 * 0.044715) * (zc * zc))))
    dz = pad_rows(cot[...].astype(F32) * slope, PAD).astype(BF16)
    dzf[m] = dz
    for i in range(1, MP):
        send(dzf.at[m], dzf.at[m], DZ, d, (m + i) % MP)
    later(dzf.at[pl.ds(0, MP - 1)], DZ)
    dz2[0] = dz[:, :128]
    dz2[1] = dz[:, 128:]
    to_columns(dz2, dz_g, DZ_G)
    mixed[...] = (zc * cdf).astype(BF16)
    emit(0, mixed, o_mixed)
    got(dzf.at[pl.ds(0, MP - 1)], DZ)

    dagg = dot_nt(dzf[0], w_neigh[:, 0:COLS])
    for j in range(1, MP):
        dagg = dagg + dot_nt(dzf[j], w_neigh[:, j * COLS : (j + 1) * COLS])
    msg = (dagg / cnt[...]).astype(BF16)
    m2[0:PAD, :] = msg[:, :128]
    m2[PAD : 2 * PAD, :] = msg[:, 128:]
    sbuf2[...] = dot(ght[...], m2[...]).astype(BF16).reshape(DP, SLOT, 128)
    to_dp(sbuf2, rbuf2, BACK)
    own = dot_nt(dzf[0], w_self[:, 0:COLS])
    for j in range(1, MP):
        own = own + dot_nt(dzf[j], w_self[:, j * COLS : (j + 1) * COLS])

    got_columns(dz_g, DZ_G)
    got(emb_g.at[pl.ds(0, NG - 1)], EMB_G)
    got(agg_g.at[pl.ds(0, NG - 1)], AGG_G)
    rhs = dz_g[...].reshape(NG * PAD, 128)
    sn_s[:, 0] = dot_tn(emb_g[...].reshape(NG * PAD, COLS), rhs).astype(BF16).reshape(NZ, PAD, 128)
    sn_s[:, 1] = dot_tn(agg_g[...].reshape(NG * PAD, COLS), rhs).astype(BF16).reshape(NZ, PAD, 128)
    scatter_z(sn_s, sn_r, SN_RS)

    got(rbuf2.at[pl.ds(0, DP - 1)], BACK)
    two = dot(sel_t[...], rbuf2[...].reshape(DP * SLOT, 128))
    grad = (own + jnp.concatenate([two[:PAD], two[PAD:]], axis=1)).astype(BF16)
    ng2[0] = grad[:, :128]
    ng2[1] = grad[:, 128:]
    to_columns(ng2, ng_g, NG_G)
    ngrad[...] = grad[:NODE]
    emit(1, ngrad, o_ngrad)

    factor = 1.0 / math.sqrt(NODE * DP)

    def z_total(buf):
        total = buf[0].astype(F32)
        for i in range(1, NZ):
            total = total + buf[i].astype(F32)
        return (total * factor).astype(BF16)

    got(sn_r.at[pl.ds(0, NZ - 1)], SN_RS)
    fin_sn[g, z] = z_total(sn_r)
    gather_z(fin_sn, SN_AG)

    got(pool_g.at[pl.ds(0, NG - 1)], POOL_G)
    got_columns(ng_g, NG_G)
    out = dot_tn(pool_g[...].reshape(NG * PAD, COLS), ng_g[...].reshape(NG * PAD, 128))
    out_s[...] = out.astype(BF16).reshape(NZ, PAD, 128)
    scatter_z(out_s, out_r, OUT_RS)

    got(fin_sn.at[0, pl.ds(0, NZ - 1)], SN_AG)
    y_sends(fin_sn, 0)

    got(out_r.at[pl.ds(0, NZ - 1)], OUT_RS)
    fin_out[g, z] = z_total(out_r)
    gather_z(fin_out, OUT_AG)

    def forward(fin, first):
        for i in range(1, NY):
            at = ((y + NY - i) % NY) * 2 + c
            y_copy(fin, at, y, first + i - 1).wait_recv()
            copy = c_copy(fin, at, (first // 3) * 4 + i)
            copy.start()
            pending.append(copy.wait_send)

    forward(fin_sn, 0)
    got(fin_out.at[0, pl.ds(0, NZ - 1)], OUT_AG)
    y_sends(fin_out, 3)

    for i in range(NY):
        c_copy(fin_sn, ((y + NY - i) % NY) * 2 + 1 - c, i).wait_recv()
    emit(2, fin_sn, o_sn)

    forward(fin_out, 3)
    for i in range(NY):
        c_copy(fin_out, ((y + NY - i) % NY) * 2 + 1 - c, 4 + i).wait_recv()
    emit(3, fin_out, o_out)

    for wait in pending:
        wait()


def step(texts, w_qkv, w_out, w_self, w_neigh, ids, cot):
    anywhere = pl.BlockSpec(memory_space=pl.ANY)
    b, f = (lambda *shape: pltpu.VMEM(shape, BF16)), (lambda *shape: pltpu.VMEM(shape, F32))
    blocks = b(DP, SLOT, 128)
    return pl.pallas_call(
        step_kernel,
        out_shape=[
            jax.ShapeDtypeStruct((NODE, COLS), BF16),
            jax.ShapeDtypeStruct((NODE, COLS), BF16),
            jax.ShapeDtypeStruct((NG, NZ, 2, PAD, 128), BF16),
            jax.ShapeDtypeStruct((NG, NZ, PAD, 128), BF16),
        ],
        in_specs=[anywhere] * 7,
        out_specs=[anywhere] * 4,
        scratch_shapes=[
            b(NODE, COLS),
            b(NODE, COLS),
            b(NG, NZ, 2, PAD, 128),
            b(NG, NZ, PAD, 128),
            b(NODE, 128, WIDTH),
            b(WIDTH, 3 * COLS),
            b(WIDTH, 3 * COLS),
            b(TEXTS * 128, 3 * COLS),
            b(COLS, WIDTH),
            b(COLS, WIDTH),
            b(COLS, WIDTH),
            pltpu.VMEM(ids.shape, jnp.int32),
            b(NODE, COLS),
            f(NODE, COLS),
            f(NODE, COLS),
            b(PAD, COLS),
            blocks,
            b(2 * PAD, DP * SLOT),
            b(DP * SLOT, 128),
            f(PAD, COLS),
            blocks,
            blocks,
            blocks,
            blocks,
            blocks,
            b(2 * PAD, DP * SLOT),
            f(MP, NODE, COLS),
            f(MP, NODE, COLS),
            f(MP, NODE, COLS),
            f(MP, NODE, COLS),
            b(128, 128),
            b(128, 128),
            b(NG, PAD, COLS),
            b(NG, PAD, COLS),
            b(NG, PAD, COLS),
            b(MP, PAD, COLS),
            b(2, PAD, 128),
            b(NG, PAD, 128),
            b(2, PAD, 128),
            b(NG, PAD, 128),
            b(NZ, 2, PAD, 128),
            b(NZ, 2, PAD, 128),
            b(NZ, PAD, 128),
            b(NZ, PAD, 128),
            pltpu.SemaphoreType.DMA((NODE // TEXTS,)),
            pltpu.SemaphoreType.DMA((6,)),
            pltpu.SemaphoreType.DMA((4,)),
            pltpu.SemaphoreType.DMA((15,)),
            pltpu.SemaphoreType.DMA((15,)),
            pltpu.SemaphoreType.DMA((6,)),
            pltpu.SemaphoreType.DMA((6,)),
            pltpu.SemaphoreType.DMA((8,)),
            pltpu.SemaphoreType.DMA((8,)),
        ],
        compiler_params=pltpu.CompilerParams(
            collective_id=0, has_side_effects=True, vmem_limit_bytes=VMEM_LIMIT
        ),
        cost_estimate=pl.CostEstimate(flops=7 * 10**9, bytes_accessed=12 * 10**6, transcendentals=1600000),
    )(texts, w_qkv, w_out, w_self, w_neigh, ids, cot)


def finish_kernel(mixed, ngrad, sn, out, o_mixed, o_ngrad, o_self, o_neigh, o_out, small, fin_sn, fin_out, wide, isem, sem):
    loads = [
        pltpu.make_async_copy(src, dst, isem.at[k])
        for k, (src, dst) in enumerate([(sn, fin_sn), (out, fin_out), (mixed, small.at[0]), (ngrad, small.at[1])])
    ]
    for copy in loads:
        copy.start()
    stores = []

    def store(k, src, dst):
        copy = pltpu.make_async_copy(src, dst, sem.at[k])
        copy.start()
        stores.append(copy)

    for k, dst in enumerate((o_self, o_neigh, o_out)):
        if k != 1:
            loads[k // 2].wait()
        for j in range(NG):
            block = fin_sn[j, :, k] if k < 2 else fin_out[j]
            wide[k, :, j * 128 : j * 128 + 128] = block.reshape(COLS, 128).astype(F32)
        store(k, wide.at[k], dst)
    for k, dst in enumerate((o_mixed, o_ngrad)):
        loads[2 + k].wait()
        store(3 + k, small.at[k], dst)
    for copy in stores:
        copy.wait()


def finish(mixed, ngrad, fin_sn, fin_out):
    anywhere = pl.BlockSpec(memory_space=pl.ANY)
    return pl.pallas_call(
        finish_kernel,
        out_shape=[
            jax.ShapeDtypeStruct((NODE, COLS), BF16),
            jax.ShapeDtypeStruct((NODE, COLS), BF16),
            jax.ShapeDtypeStruct((COLS, WIDTH), F32),
            jax.ShapeDtypeStruct((COLS, WIDTH), F32),
            jax.ShapeDtypeStruct((COLS, WIDTH), F32),
        ],
        in_specs=[anywhere] * 4,
        out_specs=[anywhere] * 5,
        scratch_shapes=[
            pltpu.VMEM((2, NODE, COLS), BF16),
            pltpu.VMEM((NG, NZ, 2, PAD, 128), BF16),
            pltpu.VMEM((NG, NZ, PAD, 128), BF16),
            pltpu.VMEM((3, COLS, WIDTH), F32),
            pltpu.SemaphoreType.DMA((4,)),
            pltpu.SemaphoreType.DMA((5,)),
        ],
        compiler_params=pltpu.CompilerParams(vmem_limit_bytes=VMEM_LIMIT),
        cost_estimate=pl.CostEstimate(flops=0, bytes_accessed=5 * 10**6, transcendentals=0),
    )(mixed, ngrad, fin_sn, fin_out)


def per_device(texts, w_qkv, w_out, w_self, w_neigh, neighbours, cotangent):
    return tuple(finish(*step(texts, w_qkv, w_out, w_self, w_neigh, neighbours.T, cotangent)))


def solution(mesh):
    return jax.shard_map(
        per_device,
        mesh=mesh,
        in_specs=(
            P("dp", None, None),
            P(None, "mp"),
            P("mp", None),
            P("mp", None),
            P("mp", None),
            P("dp", None),
            P("dp", "mp"),
        ),
        out_specs=(P("dp", "mp"), P("dp", "mp"), P("mp", None), P("mp", None), P("mp", None)),
        check_vma=False,
    )
```

```python
import math

import jax
import jax.numpy as jnp
from jax import lax
from jax.experimental import pallas as pl
from jax.experimental.pallas import tpu as pltpu
from jax.sharding import PartitionSpec as P

MESH = pl.DeviceIdType.MESH
F32, BF16 = jnp.float32, jnp.bfloat16
HD = 64
NODE = 24
PAD = 32
DP, MP, NZ, NG, NY = 64, 4, 8, 8, 4
COLS, WIDTH = 256, 1024
SLOT = 16
EMPTY = 120.0
FAR_FIRST = (4, 3, 5, 2, 6, 1, 7, 0)
VMEM_LIMIT = 60 * 2**20
TEXTS = 8


def dot(a, b):
    return jnp.dot(a, b, preferred_element_type=F32)


def dot_nt(a, b):
    return lax.dot_general(a, b, (((1,), (1,)), ((), ())), preferred_element_type=F32)


def dot_tn(a, b):
    return lax.dot_general(a, b, (((0,), (0,)), ((), ())), preferred_element_type=F32)


def iota(shape, dim):
    return lax.broadcasted_iota(jnp.int32, shape, dim)


def pad_rows(x, rows):
    return jnp.concatenate([x, jnp.zeros((rows - x.shape[0], x.shape[1]), x.dtype)], axis=0)


def routing(ids_ref, want, gh, ght, cnt_out):
    ids = jnp.transpose(ids_ref[...].astype(F32))
    own = jnp.floor((ids + 0.5) * (1.0 / NODE))
    loc = ids - NODE * own
    live = ids >= 0.0
    cnt = jnp.maximum(jnp.sum(live.astype(F32), axis=1, keepdims=True), 1.0)
    cnt_out[...] = jnp.concatenate(
        [jnp.broadcast_to(cnt, (NODE, COLS)), jnp.ones((PAD - NODE, COLS), F32)], axis=0
    )
    fan = ids.shape[1]
    groups = iota((NODE, DP), 1).astype(F32)
    hots = [(own[:, f : f + 1] == groups).astype(F32) for f in range(fan)]
    total = hots[0]
    for f in range(1, fan):
        total = total + hots[f]
    lower = (iota((NODE, NODE), 1) < iota((NODE, NODE), 0)).astype(BF16)
    run = dot(lower, total.astype(BF16))
    spots = iota((NODE, DP * SLOT), 1).astype(F32)
    left = jnp.zeros((NODE, DP * SLOT), F32)
    right = jnp.zeros((NODE, DP * SLOT), F32)
    names = jnp.zeros((NODE, DP * SLOT), F32)
    for f in range(fan):
        rank = jnp.sum(hots[f] * run, axis=1, keepdims=True)
        run = run + hots[f]
        at = jnp.where(live[:, f : f + 1], own[:, f : f + 1] * SLOT + rank, -1000.0)
        name = loc[:, f : f + 1]
        is_left = spots == at
        is_right = spots == at + 8.0
        left = left + is_left.astype(F32)
        right = right + is_right.astype(F32)
        names = names + jnp.where(is_left, name - EMPTY, 0.0)
        names = names + jnp.where(is_right, name + (PAD - EMPTY), 0.0)
    gap = jnp.zeros((PAD - NODE, DP * SLOT), F32)
    both = jnp.concatenate([left, gap, right, gap], axis=0)
    gh[...] = both.astype(BF16)
    ght[...] = jnp.transpose(pad_rows(both, 128)).astype(BF16)
    spread = jnp.transpose(pad_rows(names, 128)).astype(BF16)
    want[...] = (dot(spread, jnp.ones((128, 128), BF16)) + EMPTY).astype(BF16).reshape(DP, SLOT, 128)


def order_columns(w, wp):
    low = iota((1, 128), 1) < HD
    for pair in range(2):
        base = pair * 384
        at = pair * 128
        a = w[:, base : base + 128].astype(F32)
        b = w[:, base + 128 : base + 256].astype(F32)
        c = w[:, base + 256 : base + 384].astype(F32)
        wp[:, at : at + 128] = jnp.where(low, a, b).astype(BF16)
        wp[:, 256 + at : 384 + at] = pltpu.roll(jnp.where(low, c, a), HD, 1).astype(BF16)
        wp[:, 512 + at : 640 + at] = jnp.where(low, b, c).astype(BF16)


def attend(qkv):
    low = iota((1, 128), 1) < HD
    scale = 1.0 / (math.sqrt(HD) * math.log(2.0))
    zero = jnp.zeros((), BF16)
    texts = []
    for t in range(TEXTS):
        rows = slice(t * 128, t * 128 + 128)
        parts = []
        for pair in range(2):
            at = pair * 128
            qt = qkv[rows, at : at + 128]
            kt = qkv[rows, 256 + at : 384 + at]
            vt = qkv[rows, 512 + at : 640 + at].astype(F32)
            two = jnp.concatenate([jnp.where(low, qt, zero), jnp.where(low, zero, qt)], axis=0)
            s = dot_nt(kt, two)
            e = jnp.exp2((s - jnp.max(s, axis=0, keepdims=True)) * scale)
            p = (e * (1.0 / jnp.sum(e, axis=0, keepdims=True))).astype(BF16).astype(F32)
            first = jnp.sum(p[:, :128], axis=1, keepdims=True)
            second = jnp.sum(p[:, 128:], axis=1, keepdims=True)
            parts.append(jnp.sum(jnp.where(low, first, second) * vt, axis=0, keepdims=True))
        texts.append(jnp.concatenate(parts, axis=1))
    return jnp.concatenate(texts, axis=0) * (1.0 / 128)


ASK, POOL_SUM, ROWS, POOL_ROWS, EMB_G, POOL_G, AGG_G, AGP_G, Z_ALL, COT, DZ_G, BACK, FACT = range(13)
SN_RS, OUT_RS = range(13, 15)


def step_kernel(
    texts_in, qkv_in, out_in, self_in, neigh_in, ids_in, cot_in,
    o_mixed, o_ngrad, o_sn, o_out,
    mixed, ngrad, fin_sn, fin_out, tx, wq, wp, qkv, w_out, w_self, w_neigh, ids, cot, acc, tmean, pooled, want, gh, ght, cnt,
    asked, sel, sbufp, rbufp, sbuf, rbuf, sbuf2, rbuf2, sel_t, part, sums, cots, zsend, zall, full, e2, m2,
    emb_g, pool_g, agg_g, agp_g, dz2, dz_g, fact, fact_g, sn_s, sn_r, out_s, out_r,
    tsem, lsem, osem, ssem, rsem, z_s, z_r, y_s, y_r, c_s, c_r,
):
    m, d = lax.axis_index("mp"), lax.axis_index("dp")
    z, g = d // NG, d % NG
    y, c = g // 2, g % 2
    is_diag = (g // 2) == m

    def send(src, dst, phase, dp, mp):
        pltpu.make_async_remote_copy(
            src_ref=src, dst_ref=dst, send_sem=ssem.at[phase], recv_sem=rsem.at[phase],
            device_id=(dp, mp), device_id_type=MESH,
        ).start()

    def got(ref, phase):
        pltpu.make_async_copy(ref, ref, rsem.at[phase]).wait()

    def sent(ref, phase):
        pltpu.make_async_copy(ref, ref, ssem.at[phase]).wait()

    pending = []

    def emit(k, src, dst):
        copy = pltpu.make_async_copy(src, dst, osem.at[k])
        copy.start()
        pending.append(copy.wait)

    def later(ref, phase):
        pending.append(lambda: sent(ref, phase))

    def over(count, body):
        def step(i, carry):
            body(i)
            return carry

        lax.fori_loop(1, count, step, 0)

    def to_dp(src, dst, phase, offsets=FAR_FIRST):
        for k in offsets:

            def one(i, carry):
                to = ((z + k) % NZ) * NG + (g + i) % NG
                send(src.at[to], dst.at[d], phase, to, m)
                return carry

            lax.fori_loop(1 if k == 0 else 0, NG, one, 0)
        if offsets[-1] == 0:
            dst[d] = src[d]
            later(dst.at[pl.ds(0, DP - 1)], phase)

    def to_mp(src, dst, phase):
        for i in range(1, MP):
            to = (m + i) % MP
            send(src.at[to], dst.at[m], phase, d, to)
        dst[m] = src[m]
        later(dst.at[pl.ds(0, MP - 1)], phase)

    def share_mp(src, dst, phase):
        for i in range(1, MP):
            send(src, dst.at[m], phase, d, (m + i) % MP)
        later(dst.at[pl.ds(0, MP - 1)], phase)

    def to_group(block, phase):
        for i in range(1, NG):
            send(block.at[g], block.at[g], phase, z * NG + (g + i) % NG, m)
        later(block.at[pl.ds(0, NG - 1)], phase)

    def to_columns(src, dst, phase):
        def one(i, carry):
            mp, half = i // 2, i % 2
            at = 2 * m + half
            here = jnp.logical_and(mp == m, at == g)

            @pl.when(jnp.logical_not(here))
            def _():
                send(src.at[half], dst.at[g], phase, z * NG + at, mp)

            @pl.when(here)
            def _():
                dst[g] = src[half]

            return carry

        lax.fori_loop(0, 2 * MP, one, 0)
        pending.append(lambda: sent_columns(dst, phase))

    def got_columns(dst, phase):
        @pl.when(is_diag)
        def _():
            got(dst.at[pl.ds(0, NG - 1)], phase)

        @pl.when(jnp.logical_not(is_diag))
        def _():
            got(dst, phase)

    def sent_columns(dst, phase):
        @pl.when(is_diag)
        def _():
            sent(dst.at[pl.ds(0, NG - 1)], phase)

        @pl.when(jnp.logical_not(is_diag))
        def _():
            sent(dst, phase)

    def scatter_z(src, dst, phase):
        for i in range(1, NZ):
            to = (z + i) % NZ
            send(src.at[to], dst.at[z], phase, to * NG + g, m)
        dst[z] = src[z]
        later(dst.at[pl.ds(0, NZ - 1)], phase)

    def z_copy(fin, at, to, k, which):
        return pltpu.make_async_remote_copy(
            src_ref=fin.at[g, at], dst_ref=fin.at[g, at], send_sem=z_s.at[which, k], recv_sem=z_r.at[which, k],
            device_id=(to * NG + g, m), device_id_type=MESH,
        )

    def along_y(fin, at, which):
        for i in range(1, NY):
            pltpu.make_async_remote_copy(
                src_ref=fin.at[g, at], dst_ref=fin.at[g, at], send_sem=y_s.at[which, i], recv_sem=y_r.at[which, i],
                device_id=(z * NG + ((y + i) % NY) * 2 + c, m), device_id_type=MESH,
            ).start()

    def c_copy(fin, at, k, which):
        return pltpu.make_async_remote_copy(
            src_ref=fin.at[at], dst_ref=fin.at[at], send_sem=c_s.at[which, k], recv_sem=c_r.at[which, k],
            device_id=(z * NG + y * 2 + 1 - c, m), device_id_type=MESH,
        )

    def start_gather(fin, which):
        for k in FAR_FIRST[:-1]:
            copy = z_copy(fin, z, (z + k) % NZ, k, which)
            copy.start()
            pending.append(copy.wait_send)
        along_y(fin, z, which)

    def pass_along_y(fin, which):
        for k in reversed(FAR_FIRST[:-1]):
            at = (z + NZ - k) % NZ
            z_copy(fin, at, z, k, which).wait_recv()
            along_y(fin, at, which)
        own = c_copy(fin, g, 0, which)
        own.start()
        pending.append(own.wait_send)
        for i in range(1, NY):
            pending.append(pltpu.make_async_copy(fin.at[g], fin.at[g], y_s.at[which, i]).wait)

    def pass_to_core(fin, which):
        for i in range(1, NY):
            at = ((y + NY - i) % NY) * 2 + c
            pltpu.make_async_copy(fin.at[at], fin.at[at], y_r.at[which, i]).wait()
            copy = c_copy(fin, at, i, which)
            copy.start()
            pending.append(copy.wait_send)

    def end_gather(fin, which):
        for i in range(NY):
            c_copy(fin, ((y + NY - i) % NY) * 2 + 1 - c, i, which).wait_recv()

    weight = pltpu.make_async_copy(qkv_in, wq, lsem.at[0])
    names_in = pltpu.make_async_copy(ids_in, ids, lsem.at[1])
    names_in.start()
    weight.start()
    chunks = NODE // TEXTS

    def chunk(i):
        rows = pl.ds(i * TEXTS, TEXTS)
        return pltpu.make_async_copy(texts_in.at[rows], tx.at[rows], tsem.at[i])

    for i in range(chunks):
        chunk(i).start()
    others = [
        pltpu.make_async_copy(src, dst, lsem.at[2 + i])
        for i, (src, dst) in enumerate(
            [(out_in, w_out), (self_in, w_self), (neigh_in, w_neigh), (cot_in, cot)]
        )
    ]
    for copy in others:
        copy.start()

    bar = pltpu.get_barrier_semaphore()
    over(DP, lambda i: pl.semaphore_signal(bar, inc=1, device_id=((d + i) % DP, m), device_id_type=MESH))
    for i in range(1, MP):
        pl.semaphore_signal(bar, inc=1, device_id=(d, (m + i) % MP), device_id_type=MESH)

    def greet(i, carry):
        @pl.when(jnp.logical_not(jnp.logical_and(is_diag, i == g)))
        def _():
            pl.semaphore_signal(bar, inc=1, device_id=(z * NG + i, g // 2), device_id_type=MESH)

        return carry

    lax.fori_loop(0, NG, greet, 0)

    names_in.wait()
    routing(ids, want, gh, ght, cnt)
    e2[...] = jnp.zeros_like(e2)
    m2[...] = jnp.zeros_like(m2)
    weight.wait()
    order_columns(wq, wp)

    def work(i, carry):
        chunk(i).wait()
        rows = pl.ds(pl.multiple_of(i * TEXTS, TEXTS), TEXTS)
        qkv[...] = dot(tx[rows].reshape(TEXTS * 128, WIDTH), wp[...]).astype(BF16)
        acc[rows, :] = attend(qkv)
        mine = tx[rows, :, pl.ds(pl.multiple_of(m * COLS, COLS), COLS)]
        tmean[rows, :] = jnp.sum(mine.astype(F32), axis=1) * (1.0 / 128)

        @pl.when(i == 0)
        def _():
            pl.semaphore_wait(bar, DP - 1 + MP - 1 + 2 * MP - is_diag.astype(jnp.int32))
            to_dp(want, asked, ASK)

        return carry

    lax.fori_loop(0, chunks, work, 0)
    for copy in others:
        copy.wait()
    pooled[...] = pad_rows(acc[...], PAD).astype(BF16)
    pool_g[g] = pooled[...]
    first = dot(pooled[...], w_out[...])
    for j in range(MP):
        part[j] = first[:NODE, j * COLS : (j + 1) * COLS]

    def halves(dst, x):
        dst[0:PAD, :] = x[:, :128]
        dst[PAD : 2 * PAD, :] = x[:, 128:]

    def whole(x):
        return jnp.concatenate([x[:PAD], x[PAD : 2 * PAD]], axis=1)

    def rows_of(onehot, x):
        return dot(onehot, x).astype(BF16).reshape(DP, SLOT, 128)

    to_mp(part, sums, POOL_SUM)
    cots[m] = pad_rows(cot[...], PAD)
    share_mp(cots.at[m], cots, COT)
    got(asked.at[pl.ds(0, DP - 1)], ASK)
    names = asked[...].reshape(DP * SLOT, 128).astype(F32)
    hot = (names == iota((DP * SLOT, 128), 1).astype(F32)).astype(F32)
    sel[...] = hot.astype(BF16)
    halves(m2, pooled[...])
    sbufp[...] = rows_of(sel[...], m2[...])
    sel_t[...] = jnp.transpose(hot)[: 2 * PAD].astype(BF16)
    got(sums.at[pl.ds(0, MP - 1)], POOL_SUM)
    embed = tmean[...] + (sums[0] + sums[1] + sums[2] + sums[3])
    embed = pad_rows(embed, PAD).astype(BF16)
    halves(e2, embed)
    emb_g[g] = embed

    sbuf[...] = rows_of(sel[...], e2[...])
    to_dp(sbuf, rbuf, ROWS)
    to_dp(sbufp, rbufp, POOL_ROWS)
    zself = dot(embed, w_self[...])
    to_group(emb_g, EMB_G)
    to_group(pool_g, POOL_G)
    got(rbuf.at[pl.ds(0, DP - 1)], ROWS)
    agg = (whole(dot(gh[...], rbuf[...].reshape(DP * SLOT, 128))) / cnt[...]).astype(BF16)
    zfull = zself + dot(agg, w_neigh[...])
    zsend[...] = zfull.astype(BF16)
    share_mp(zsend, zall, Z_ALL)
    zall[m] = jnp.zeros((PAD, WIDTH), BF16)
    agg_g[g] = agg
    to_group(agg_g, AGG_G)
    got(cots.at[pl.ds(0, MP - 1)], COT)
    got(zall.at[pl.ds(0, MP - 1)], Z_ALL)
    zc = zfull
    for j in range(MP):
        zc = zc + zall[j].astype(F32)

    root = math.sqrt(2.0 / math.pi)
    th = jnp.tanh(root * (zc + 0.044715 * (zc * zc * zc)))
    cdf = 0.5 * (1.0 + th)
    slope = cdf + zc * (0.5 * (1.0 - th * th) * (root * (1.0 + (3 * 0.044715) * (zc * zc))))
    dz = (jnp.concatenate([cots[j] for j in range(MP)], axis=1).astype(F32) * slope).astype(BF16)
    for j in range(NG):
        dz2[j] = dz[:, j * 128 : j * 128 + 128]
    for i in range(1, NG):
        to = (g + i) % NG
        send(dz2.at[to], dz_g.at[g], DZ_G, z * NG + to, m)
    dz_g[g] = dz2[g]
    later(dz_g.at[pl.ds(0, NG - 1)], DZ_G)

    own = dot_nt(dz, w_self[...])
    msg = (dot_nt(dz, w_neigh[...]) / cnt[...]).astype(BF16)
    for k, x in enumerate((own.astype(BF16), msg)):
        fact[0, k] = x[:, :128]
        fact[1, k] = x[:, 128:]
    to_columns(fact, fact_g, FACT)
    full[...] = zc * cdf
    mixed[...] = full[:NODE, pl.ds(pl.multiple_of(m * COLS, COLS), COLS)].astype(BF16)
    emit(0, mixed, o_mixed)

    def grad_of(lhs, rhs):
        return dot_tn(lhs[...].reshape(NG * PAD, COLS), rhs.reshape(NG * PAD, 128))

    def rounded(x):
        return x.astype(BF16).reshape(NZ, PAD, 128)

    got(dz_g.at[pl.ds(0, NG - 1)], DZ_G)
    got(emb_g.at[pl.ds(0, NG - 1)], EMB_G)
    got(agg_g.at[pl.ds(0, NG - 1)], AGG_G)
    sn_s[:, 0] = rounded(grad_of(emb_g, dz_g[...]))
    sn_s[:, 1] = rounded(grad_of(agg_g, dz_g[...]))
    scatter_z(sn_s, sn_r, SN_RS)

    got(rbufp.at[pl.ds(0, DP - 1)], POOL_ROWS)
    agp_g[g] = whole(dot(gh[...], rbufp[...].reshape(DP * SLOT, 128))).astype(BF16)
    to_group(agp_g, AGP_G)

    halves(m2, msg)
    sbuf2[...] = rows_of(ght[...], m2[...])

    factor = 1.0 / math.sqrt(NODE * DP)

    def z_total(buf):
        total = buf[0].astype(F32)
        for i in range(1, NZ):
            total = total + buf[i].astype(F32)
        return (total * factor).astype(BF16)

    got(pool_g.at[pl.ds(0, NG - 1)], POOL_G)
    got(agp_g.at[pl.ds(0, NG - 1)], AGP_G)
    got_columns(fact_g, FACT)
    out_s[...] = rounded(grad_of(pool_g, fact_g[:, 0]) + grad_of(agp_g, fact_g[:, 1]))
    scatter_z(out_s, out_r, OUT_RS)
    got(sn_r.at[pl.ds(0, NZ - 1)], SN_RS)
    fin_sn[g, z] = z_total(sn_r)
    start_gather(fin_sn, 0)

    got(out_r.at[pl.ds(0, NZ - 1)], OUT_RS)
    fin_out[g, z] = z_total(out_r)
    start_gather(fin_out, 1)
    pass_along_y(fin_sn, 0)
    to_dp(sbuf2, rbuf2, BACK)
    pass_along_y(fin_out, 1)
    pass_to_core(fin_sn, 0)

    got(rbuf2.at[pl.ds(0, DP - 1)], BACK)
    grad = own + whole(dot(sel_t[...], rbuf2[...].reshape(DP * SLOT, 128)))
    ngrad[...] = grad[:NODE].astype(BF16)
    emit(1, ngrad, o_ngrad)
    end_gather(fin_sn, 0)
    emit(2, fin_sn, o_sn)
    pass_to_core(fin_out, 1)
    end_gather(fin_out, 1)
    emit(3, fin_out, o_out)

    for wait in pending:
        wait()


def step(texts, w_qkv, w_out, w_self, w_neigh, ids, cot):
    anywhere = pl.BlockSpec(memory_space=pl.ANY)
    b, f = (lambda *shape: pltpu.VMEM(shape, BF16)), (lambda *shape: pltpu.VMEM(shape, F32))
    blocks = b(DP, SLOT, 128)
    return pl.pallas_call(
        step_kernel,
        out_shape=[
            jax.ShapeDtypeStruct((NODE, COLS), BF16),
            jax.ShapeDtypeStruct((NODE, COLS), BF16),
            jax.ShapeDtypeStruct((NG, NZ, 2, PAD, 128), BF16),
            jax.ShapeDtypeStruct((NG, NZ, PAD, 128), BF16),
        ],
        in_specs=[anywhere] * 7,
        out_specs=[anywhere] * 4,
        scratch_shapes=[
            b(NODE, COLS),
            b(NODE, COLS),
            b(NG, NZ, 2, PAD, 128),
            b(NG, NZ, PAD, 128),
            b(NODE, 128, WIDTH),
            b(WIDTH, 3 * COLS),
            b(WIDTH, 3 * COLS),
            b(TEXTS * 128, 3 * COLS),
            b(COLS, WIDTH),
            b(COLS, WIDTH),
            b(COLS, WIDTH),
            pltpu.VMEM(ids.shape, jnp.int32),
            b(NODE, COLS),
            f(NODE, COLS),
            f(NODE, COLS),
            b(PAD, COLS),
            blocks,
            b(2 * PAD, DP * SLOT),
            b(DP * SLOT, 128),
            f(PAD, COLS),
            blocks,
            b(DP * SLOT, 128),
            blocks,
            blocks,
            blocks,
            blocks,
            blocks,
            blocks,
            b(2 * PAD, DP * SLOT),
            f(MP, NODE, COLS),
            f(MP, NODE, COLS),
            b(MP, PAD, COLS),
            b(PAD, WIDTH),
            b(MP, PAD, WIDTH),
            f(PAD, WIDTH),
            b(128, 128),
            b(128, 128),
            b(NG, PAD, COLS),
            b(NG, PAD, COLS),
            b(NG, PAD, COLS),
            b(NG, PAD, COLS),
            b(NG, PAD, 128),
            b(NG, PAD, 128),
            b(2, 2, PAD, 128),
            b(NG, 2, PAD, 128),
            b(NZ, 2, PAD, 128),
            b(NZ, 2, PAD, 128),
            b(NZ, PAD, 128),
            b(NZ, PAD, 128),
            pltpu.SemaphoreType.DMA((NODE // TEXTS,)),
            pltpu.SemaphoreType.DMA((6,)),
            pltpu.SemaphoreType.DMA((4,)),
            pltpu.SemaphoreType.DMA((15,)),
            pltpu.SemaphoreType.DMA((15,)),
            pltpu.SemaphoreType.DMA((2, NZ)),
            pltpu.SemaphoreType.DMA((2, NZ)),
            pltpu.SemaphoreType.DMA((2, NY)),
            pltpu.SemaphoreType.DMA((2, NY)),
            pltpu.SemaphoreType.DMA((2, NY)),
            pltpu.SemaphoreType.DMA((2, NY)),
        ],
        compiler_params=pltpu.CompilerParams(
            collective_id=0, has_side_effects=True, vmem_limit_bytes=VMEM_LIMIT
        ),
        cost_estimate=pl.CostEstimate(flops=7 * 10**9, bytes_accessed=12 * 10**6, transcendentals=1600000),
    )(texts, w_qkv, w_out, w_self, w_neigh, ids, cot)


def finish_kernel(mixed, ngrad, sn, out, o_mixed, o_ngrad, o_self, o_neigh, o_out, small, fin_sn, fin_out, wide, isem, sem):
    loads = [
        pltpu.make_async_copy(src, dst, isem.at[k])
        for k, (src, dst) in enumerate([(sn, fin_sn), (out, fin_out), (mixed, small.at[0]), (ngrad, small.at[1])])
    ]
    for copy in loads:
        copy.start()
    stores = []

    def store(k, src, dst):
        copy = pltpu.make_async_copy(src, dst, sem.at[k])
        copy.start()
        stores.append(copy)

    for k, dst in enumerate((o_self, o_neigh, o_out)):
        if k != 1:
            loads[k // 2].wait()
        for j in range(NG):
            block = fin_sn[j, :, k] if k < 2 else fin_out[j]
            wide[k, :, j * 128 : j * 128 + 128] = block.reshape(COLS, 128).astype(F32)
        store(k, wide.at[k], dst)
    for k, dst in enumerate((o_mixed, o_ngrad)):
        loads[2 + k].wait()
        store(3 + k, small.at[k], dst)
    for copy in stores:
        copy.wait()


def finish(mixed, ngrad, fin_sn, fin_out):
    anywhere = pl.BlockSpec(memory_space=pl.ANY)
    return pl.pallas_call(
        finish_kernel,
        out_shape=[
            jax.ShapeDtypeStruct((NODE, COLS), BF16),
            jax.ShapeDtypeStruct((NODE, COLS), BF16),
            jax.ShapeDtypeStruct((COLS, WIDTH), F32),
            jax.ShapeDtypeStruct((COLS, WIDTH), F32),
            jax.ShapeDtypeStruct((COLS, WIDTH), F32),
        ],
        in_specs=[anywhere] * 4,
        out_specs=[anywhere] * 5,
        scratch_shapes=[
            pltpu.VMEM((2, NODE, COLS), BF16),
            pltpu.VMEM((NG, NZ, 2, PAD, 128), BF16),
            pltpu.VMEM((NG, NZ, PAD, 128), BF16),
            pltpu.VMEM((3, COLS, WIDTH), F32),
            pltpu.SemaphoreType.DMA((4,)),
            pltpu.SemaphoreType.DMA((5,)),
        ],
        compiler_params=pltpu.CompilerParams(vmem_limit_bytes=VMEM_LIMIT),
        cost_estimate=pl.CostEstimate(flops=0, bytes_accessed=5 * 10**6, transcendentals=0),
    )(mixed, ngrad, fin_sn, fin_out)


def per_device(texts, w_qkv, w_out, w_self, w_neigh, neighbours, cotangent):
    return tuple(finish(*step(texts, w_qkv, w_out, w_self, w_neigh, neighbours.T, cotangent)))


def solution(mesh):
    return jax.shard_map(
        per_device,
        mesh=mesh,
        in_specs=(
            P("dp", None, None),
            P(None, "mp"),
            P("mp", None),
            P("mp", None),
            P("mp", None),
            P("dp", None),
            P("dp", "mp"),
        ),
        out_specs=(P("dp", "mp"), P("dp", "mp"), P("mp", None), P("mp", None), P("mp", None)),
        check_vma=False,
    )
```

```python
import math

import jax
import jax.numpy as jnp
from jax import lax
from jax.experimental import pallas as pl
from jax.experimental.pallas import tpu as pltpu
from jax.sharding import PartitionSpec as P

MESH = pl.DeviceIdType.MESH
F32, BF16 = jnp.float32, jnp.bfloat16
HD = 64
NODE = 24
PAD = 32
DP, MP, NZ, NG, NY = 64, 4, 8, 8, 4
COLS, WIDTH = 256, 1024
SLOT = 16
EMPTY = 120.0
FAR_FIRST = (4, 3, 5, 2, 6, 1, 7, 0)
VMEM_LIMIT = 60 * 2**20
TEXTS = 8


def dot(a, b):
    return jnp.dot(a, b, preferred_element_type=F32)


def dot_nt(a, b):
    return lax.dot_general(a, b, (((1,), (1,)), ((), ())), preferred_element_type=F32)


def dot_tn(a, b):
    return lax.dot_general(a, b, (((0,), (0,)), ((), ())), preferred_element_type=F32)


def iota(shape, dim):
    return lax.broadcasted_iota(jnp.int32, shape, dim)


def pad_rows(x, rows):
    return jnp.concatenate([x, jnp.zeros((rows - x.shape[0], x.shape[1]), x.dtype)], axis=0)


def routing(ids_ref, want, gh, ght, cnt_out):
    ids = jnp.transpose(ids_ref[...].astype(F32))
    own = jnp.floor((ids + 0.5) * (1.0 / NODE))
    loc = ids - NODE * own
    live = ids >= 0.0
    cnt = jnp.maximum(jnp.sum(live.astype(F32), axis=1, keepdims=True), 1.0)
    cnt_out[...] = jnp.concatenate(
        [jnp.broadcast_to(cnt, (NODE, COLS)), jnp.ones((PAD - NODE, COLS), F32)], axis=0
    )
    fan = ids.shape[1]
    groups = iota((NODE, DP), 1).astype(F32)
    hots = [(own[:, f : f + 1] == groups).astype(F32) for f in range(fan)]
    total = hots[0]
    for f in range(1, fan):
        total = total + hots[f]
    lower = (iota((NODE, NODE), 1) < iota((NODE, NODE), 0)).astype(BF16)
    run = dot(lower, total.astype(BF16))
    spots = iota((NODE, DP * SLOT), 1).astype(F32)
    left = jnp.zeros((NODE, DP * SLOT), F32)
    right = jnp.zeros((NODE, DP * SLOT), F32)
    names = jnp.zeros((NODE, DP * SLOT), F32)
    for f in range(fan):
        rank = jnp.sum(hots[f] * run, axis=1, keepdims=True)
        run = run + hots[f]
        at = jnp.where(live[:, f : f + 1], own[:, f : f + 1] * SLOT + rank, -1000.0)
        name = loc[:, f : f + 1]
        is_left = spots == at
        is_right = spots == at + 8.0
        left = left + is_left.astype(F32)
        right = right + is_right.astype(F32)
        names = names + jnp.where(is_left, name - EMPTY, 0.0)
        names = names + jnp.where(is_right, name + (PAD - EMPTY), 0.0)
    gap = jnp.zeros((PAD - NODE, DP * SLOT), F32)
    both = jnp.concatenate([left, gap, right, gap], axis=0)
    gh[...] = both.astype(BF16)
    ght[...] = jnp.transpose(pad_rows(both, 128)).astype(BF16)
    spread = jnp.transpose(pad_rows(names, 128)).astype(BF16)
    want[...] = (dot(spread, jnp.ones((128, 128), BF16)) + EMPTY).astype(BF16).reshape(DP, SLOT, 128)


def order_columns(w, wp):
    low = iota((1, 128), 1) < HD
    for pair in range(2):
        base = pair * 384
        at = pair * 128
        a = w[:, base : base + 128].astype(F32)
        b = w[:, base + 128 : base + 256].astype(F32)
        c = w[:, base + 256 : base + 384].astype(F32)
        wp[:, at : at + 128] = jnp.where(low, a, b).astype(BF16)
        wp[:, 256 + at : 384 + at] = pltpu.roll(jnp.where(low, c, a), HD, 1).astype(BF16)
        wp[:, 512 + at : 640 + at] = jnp.where(low, b, c).astype(BF16)


def attend(qkv):
    low = iota((1, 128), 1) < HD
    scale = 1.0 / (math.sqrt(HD) * math.log(2.0))
    zero = jnp.zeros((), BF16)
    texts = []
    for t in range(TEXTS):
        rows = slice(t * 128, t * 128 + 128)
        parts = []
        for pair in range(2):
            at = pair * 128
            qt = qkv[rows, at : at + 128]
            kt = qkv[rows, 256 + at : 384 + at]
            vt = qkv[rows, 512 + at : 640 + at].astype(F32)
            two = jnp.concatenate([jnp.where(low, qt, zero), jnp.where(low, zero, qt)], axis=0)
            s = dot_nt(kt, two)
            e = jnp.exp2((s - jnp.max(s, axis=0, keepdims=True)) * scale)
            p = (e * (1.0 / jnp.sum(e, axis=0, keepdims=True))).astype(BF16).astype(F32)
            first = jnp.sum(p[:, :128], axis=1, keepdims=True)
            second = jnp.sum(p[:, 128:], axis=1, keepdims=True)
            parts.append(jnp.sum(jnp.where(low, first, second) * vt, axis=0, keepdims=True))
        texts.append(jnp.concatenate(parts, axis=1))
    return jnp.concatenate(texts, axis=0) * (1.0 / 128)


ASK, POOL_SUM, ROWS, POOL_ROWS, EMB_G, POOL_G, AGG_G, AGP_G, Z_ALL, COT, DZ_G, BACK, FACT = range(13)
SN_RS, OUT_RS = range(13, 15)


def step_kernel(
    texts_in, qkv_in, out_in, self_in, neigh_in, ids_in, cot_in,
    o_mixed, o_ngrad, o_sn, o_out,
    mixed, ngrad, fin_sn, fin_out, tx, wq, wp, qkv, w_out, w_self, w_neigh, ids, cot, acc, tmean, pooled, want, gh, ght, cnt,
    asked, sel, sbufp, rbufp, sbuf, rbuf, sbuf2, rbuf2, sel_t, part, sums, cots, zsend, zall, full, e2, m2,
    emb_g, pool_g, agg_g, agp_g, dz2, dz_g, fact, fact_g, sn_s, sn_r, out_s, out_r,
    tsem, lsem, osem, ssem, rsem, z_s, z_r, y_s, y_r, c_s, c_r,
):
    m, d = lax.axis_index("mp"), lax.axis_index("dp")
    z, g = d // NG, d % NG
    y, c = g // 2, g % 2
    is_diag = (g // 2) == m

    def send(src, dst, phase, dp, mp):
        pltpu.make_async_remote_copy(
            src_ref=src, dst_ref=dst, send_sem=ssem.at[phase], recv_sem=rsem.at[phase],
            device_id=(dp, mp), device_id_type=MESH,
        ).start()

    def got(ref, phase):
        pltpu.make_async_copy(ref, ref, rsem.at[phase]).wait()

    def sent(ref, phase):
        pltpu.make_async_copy(ref, ref, ssem.at[phase]).wait()

    pending = []

    def emit(k, src, dst):
        copy = pltpu.make_async_copy(src, dst, osem.at[k])
        copy.start()
        pending.append(copy.wait)

    def later(ref, phase):
        pending.append(lambda: sent(ref, phase))

    def over(count, body):
        def step(i, carry):
            body(i)
            return carry

        lax.fori_loop(1, count, step, 0)

    def to_dp(src, dst, phase, offsets=FAR_FIRST):
        for k in offsets:

            def one(i, carry):
                to = ((z + k) % NZ) * NG + (g + i) % NG
                send(src.at[to], dst.at[d], phase, to, m)
                return carry

            lax.fori_loop(1 if k == 0 else 0, NG, one, 0)
        if offsets[-1] == 0:
            dst[d] = src[d]
            later(dst.at[pl.ds(0, DP - 1)], phase)

    def to_mp(src, dst, phase):
        for i in range(1, MP):
            to = (m + i) % MP
            send(src.at[to], dst.at[m], phase, d, to)
        dst[m] = src[m]
        later(dst.at[pl.ds(0, MP - 1)], phase)

    def share_mp(src, dst, phase):
        for i in range(1, MP):
            send(src, dst.at[m], phase, d, (m + i) % MP)
        later(dst.at[pl.ds(0, MP - 1)], phase)

    def to_group(block, phase):
        for i in range(1, NG):
            send(block.at[g], block.at[g], phase, z * NG + (g + i) % NG, m)
        later(block.at[pl.ds(0, NG - 1)], phase)

    def to_columns(src, dst, phase):
        def one(i, carry):
            mp, half = i // 2, i % 2
            at = 2 * m + half
            here = jnp.logical_and(mp == m, at == g)

            @pl.when(jnp.logical_not(here))
            def _():
                send(src.at[half], dst.at[g], phase, z * NG + at, mp)

            @pl.when(here)
            def _():
                dst[g] = src[half]

            return carry

        lax.fori_loop(0, 2 * MP, one, 0)
        pending.append(lambda: sent_columns(dst, phase))

    def got_columns(dst, phase):
        @pl.when(is_diag)
        def _():
            got(dst.at[pl.ds(0, NG - 1)], phase)

        @pl.when(jnp.logical_not(is_diag))
        def _():
            got(dst, phase)

    def sent_columns(dst, phase):
        @pl.when(is_diag)
        def _():
            sent(dst.at[pl.ds(0, NG - 1)], phase)

        @pl.when(jnp.logical_not(is_diag))
        def _():
            sent(dst, phase)

    def scatter_z(src, dst, phase):
        for i in range(1, NZ):
            to = (z + i) % NZ
            send(src.at[to], dst.at[z], phase, to * NG + g, m)
        dst[z] = src[z]
        later(dst.at[pl.ds(0, NZ - 1)], phase)

    def z_copy(fin, at, to, k, which):
        return pltpu.make_async_remote_copy(
            src_ref=fin.at[g, at], dst_ref=fin.at[g, at], send_sem=z_s.at[which, k], recv_sem=z_r.at[which, k],
            device_id=(to * NG + g, m), device_id_type=MESH,
        )

    def along_y(fin, at, which):
        for i in range(1, NY):
            pltpu.make_async_remote_copy(
                src_ref=fin.at[g, at], dst_ref=fin.at[g, at], send_sem=y_s.at[which, i], recv_sem=y_r.at[which, i],
                device_id=(z * NG + ((y + i) % NY) * 2 + c, m), device_id_type=MESH,
            ).start()

    def c_copy(fin, at, k, which):
        return pltpu.make_async_remote_copy(
            src_ref=fin.at[at], dst_ref=fin.at[at], send_sem=c_s.at[which, k], recv_sem=c_r.at[which, k],
            device_id=(z * NG + y * 2 + 1 - c, m), device_id_type=MESH,
        )

    def start_gather(fin, which):
        for k in FAR_FIRST[:-1]:
            copy = z_copy(fin, z, (z + k) % NZ, k, which)
            copy.start()
            pending.append(copy.wait_send)
        along_y(fin, z, which)

    def pass_along_y(fin, which):
        for k in reversed(FAR_FIRST[:-1]):
            at = (z + NZ - k) % NZ
            z_copy(fin, at, z, k, which).wait_recv()
            along_y(fin, at, which)
        own = c_copy(fin, g, 0, which)
        own.start()
        pending.append(own.wait_send)
        for i in range(1, NY):
            pending.append(pltpu.make_async_copy(fin.at[g], fin.at[g], y_s.at[which, i]).wait)

    def pass_to_core(fin, which):
        for i in range(1, NY):
            at = ((y + NY - i) % NY) * 2 + c
            pltpu.make_async_copy(fin.at[at], fin.at[at], y_r.at[which, i]).wait()
            copy = c_copy(fin, at, i, which)
            copy.start()
            pending.append(copy.wait_send)

    def end_gather(fin, which):
        for i in range(NY):
            c_copy(fin, ((y + NY - i) % NY) * 2 + 1 - c, i, which).wait_recv()

    weight = pltpu.make_async_copy(qkv_in, wq, lsem.at[0])
    names_in = pltpu.make_async_copy(ids_in, ids, lsem.at[1])
    names_in.start()
    weight.start()
    chunks = NODE // TEXTS

    def chunk(i):
        rows = pl.ds(i * TEXTS, TEXTS)
        return pltpu.make_async_copy(texts_in.at[rows], tx.at[rows], tsem.at[i])

    for i in range(chunks):
        chunk(i).start()
    others = [
        pltpu.make_async_copy(src, dst, lsem.at[2 + i])
        for i, (src, dst) in enumerate(
            [(out_in, w_out), (self_in, w_self), (neigh_in, w_neigh), (cot_in, cot)]
        )
    ]
    for copy in others:
        copy.start()

    bar = pltpu.get_barrier_semaphore()
    over(DP, lambda i: pl.semaphore_signal(bar, inc=1, device_id=((d + i) % DP, m), device_id_type=MESH))
    for i in range(1, MP):
        pl.semaphore_signal(bar, inc=1, device_id=(d, (m + i) % MP), device_id_type=MESH)

    def greet(i, carry):
        @pl.when(jnp.logical_not(jnp.logical_and(is_diag, i == g)))
        def _():
            pl.semaphore_signal(bar, inc=1, device_id=(z * NG + i, g // 2), device_id_type=MESH)

        return carry

    lax.fori_loop(0, NG, greet, 0)

    names_in.wait()
    routing(ids, want, gh, ght, cnt)
    e2[...] = jnp.zeros_like(e2)
    m2[...] = jnp.zeros_like(m2)
    weight.wait()
    order_columns(wq, wp)

    def work(i, carry):
        chunk(i).wait()
        rows = pl.ds(pl.multiple_of(i * TEXTS, TEXTS), TEXTS)
        qkv[...] = dot(tx[rows].reshape(TEXTS * 128, WIDTH), wp[...]).astype(BF16)
        acc[rows, :] = attend(qkv)
        mine = tx[rows, :, pl.ds(pl.multiple_of(m * COLS, COLS), COLS)]
        tmean[rows, :] = jnp.sum(mine.astype(F32), axis=1) * (1.0 / 128)

        @pl.when(i == 0)
        def _():
            pl.semaphore_wait(bar, DP - 1 + MP - 1 + 2 * MP - is_diag.astype(jnp.int32))
            to_dp(want, asked, ASK)

        return carry

    lax.fori_loop(0, chunks, work, 0)
    for copy in others:
        copy.wait()
    pooled[...] = pad_rows(acc[...], PAD).astype(BF16)
    pool_g[g] = pooled[...]
    first = dot(pooled[...], w_out[...])
    for j in range(MP):
        part[j] = first[:NODE, j * COLS : (j + 1) * COLS]

    def halves(dst, x):
        dst[0:PAD, :] = x[:, :128]
        dst[PAD : 2 * PAD, :] = x[:, 128:]

    def whole(x):
        return jnp.concatenate([x[:PAD], x[PAD : 2 * PAD]], axis=1)

    def rows_of(onehot, x):
        return dot(onehot, x).astype(BF16).reshape(DP, SLOT, 128)

    to_mp(part, sums, POOL_SUM)
    cots[m] = pad_rows(cot[...], PAD)
    share_mp(cots.at[m], cots, COT)
    got(asked.at[pl.ds(0, DP - 1)], ASK)
    names = asked[...].reshape(DP * SLOT, 128).astype(F32)
    hot = (names == iota((DP * SLOT, 128), 1).astype(F32)).astype(F32)
    sel[...] = hot.astype(BF16)
    halves(m2, pooled[...])
    sbufp[...] = rows_of(sel[...], m2[...])
    sel_t[...] = jnp.transpose(hot)[: 2 * PAD].astype(BF16)
    got(sums.at[pl.ds(0, MP - 1)], POOL_SUM)
    embed = tmean[...] + (sums[0] + sums[1] + sums[2] + sums[3])
    embed = pad_rows(embed, PAD).astype(BF16)
    halves(e2, embed)
    emb_g[g] = embed

    sbuf[...] = rows_of(sel[...], e2[...])
    to_dp(sbuf, rbuf, ROWS)
    to_dp(sbufp, rbufp, POOL_ROWS)
    zself = dot(embed, w_self[...])
    to_group(emb_g, EMB_G)
    to_group(pool_g, POOL_G)
    got(rbuf.at[pl.ds(0, DP - 1)], ROWS)
    agg = (whole(dot(gh[...], rbuf[...].reshape(DP * SLOT, 128))) / cnt[...]).astype(BF16)
    zfull = zself + dot(agg, w_neigh[...])
    zsend[...] = jnp.concatenate([zfull[:NODE, : WIDTH // 2], zfull[:NODE, WIDTH // 2 :]], axis=0).astype(BF16)
    share_mp(zsend, zall, Z_ALL)
    zall[m] = jnp.zeros((2 * NODE, WIDTH // 2), BF16)
    agg_g[g] = agg
    to_group(agg_g, AGG_G)
    got(rbufp.at[pl.ds(0, DP - 1)], POOL_ROWS)
    agp_g[g] = whole(dot(gh[...], rbufp[...].reshape(DP * SLOT, 128))).astype(BF16)
    to_group(agp_g, AGP_G)


    got(cots.at[pl.ds(0, MP - 1)], COT)
    got(zall.at[pl.ds(0, MP - 1)], Z_ALL)
    total = zall[0].astype(F32)
    for j in range(1, MP):
        total = total + zall[j].astype(F32)
    zc = zfull + pad_rows(jnp.concatenate([total[:NODE], total[NODE:]], axis=1), PAD)

    root = math.sqrt(2.0 / math.pi)
    th = jnp.tanh(root * (zc + 0.044715 * (zc * zc * zc)))
    cdf = 0.5 * (1.0 + th)
    slope = cdf + zc * (0.5 * (1.0 - th * th) * (root * (1.0 + (3 * 0.044715) * (zc * zc))))
    dz = (jnp.concatenate([cots[j] for j in range(MP)], axis=1).astype(F32) * slope).astype(BF16)
    for j in range(NG):
        dz2[j] = dz[:, j * 128 : j * 128 + 128]
    for i in range(1, NG):
        to = (g + i) % NG
        send(dz2.at[to], dz_g.at[g], DZ_G, z * NG + to, m)
    dz_g[g] = dz2[g]
    later(dz_g.at[pl.ds(0, NG - 1)], DZ_G)

    own = dot_nt(dz, w_self[...])
    msg = (dot_nt(dz, w_neigh[...]) / cnt[...]).astype(BF16)
    for k, x in enumerate((own.astype(BF16), msg)):
        fact[0, k] = x[:, :128]
        fact[1, k] = x[:, 128:]
    to_columns(fact, fact_g, FACT)
    halves(m2, msg)
    sbuf2[...] = rows_of(ght[...], m2[...])
    to_dp(sbuf2, rbuf2, BACK)
    full[...] = zc * cdf
    mixed[...] = full[:NODE, pl.ds(pl.multiple_of(m * COLS, COLS), COLS)].astype(BF16)
    emit(0, mixed, o_mixed)

    def grad_of(lhs, rhs):
        return dot_tn(lhs[...].reshape(NG * PAD, COLS), rhs.reshape(NG * PAD, 128))

    def rounded(x):
        return x.astype(BF16).reshape(NZ, PAD, 128)

    got(dz_g.at[pl.ds(0, NG - 1)], DZ_G)
    got(emb_g.at[pl.ds(0, NG - 1)], EMB_G)
    got(agg_g.at[pl.ds(0, NG - 1)], AGG_G)
    sn_s[:, 0] = rounded(grad_of(emb_g, dz_g[...]))
    sn_s[:, 1] = rounded(grad_of(agg_g, dz_g[...]))
    scatter_z(sn_s, sn_r, SN_RS)

    factor = 1.0 / math.sqrt(NODE * DP)

    def z_total(buf):
        total = buf[0].astype(F32)
        for i in range(1, NZ):
            total = total + buf[i].astype(F32)
        return (total * factor).astype(BF16)

    got(pool_g.at[pl.ds(0, NG - 1)], POOL_G)
    got(agp_g.at[pl.ds(0, NG - 1)], AGP_G)
    got_columns(fact_g, FACT)
    out_s[...] = rounded(grad_of(pool_g, fact_g[:, 0]) + grad_of(agp_g, fact_g[:, 1]))
    scatter_z(out_s, out_r, OUT_RS)
    got(sn_r.at[pl.ds(0, NZ - 1)], SN_RS)
    fin_sn[g, z] = z_total(sn_r)
    start_gather(fin_sn, 0)

    got(out_r.at[pl.ds(0, NZ - 1)], OUT_RS)
    fin_out[g, z] = z_total(out_r)
    start_gather(fin_out, 1)
    pass_along_y(fin_sn, 0)
    pass_along_y(fin_out, 1)
    pass_to_core(fin_sn, 0)

    got(rbuf2.at[pl.ds(0, DP - 1)], BACK)
    grad = own + whole(dot(sel_t[...], rbuf2[...].reshape(DP * SLOT, 128)))
    ngrad[...] = grad[:NODE].astype(BF16)
    emit(1, ngrad, o_ngrad)
    end_gather(fin_sn, 0)
    emit(2, fin_sn, o_sn)
    pass_to_core(fin_out, 1)
    end_gather(fin_out, 1)
    emit(3, fin_out, o_out)

    for wait in pending:
        wait()


def step(texts, w_qkv, w_out, w_self, w_neigh, ids, cot):
    anywhere = pl.BlockSpec(memory_space=pl.ANY)
    b, f = (lambda *shape: pltpu.VMEM(shape, BF16)), (lambda *shape: pltpu.VMEM(shape, F32))
    blocks = b(DP, SLOT, 128)
    return pl.pallas_call(
        step_kernel,
        out_shape=[
            jax.ShapeDtypeStruct((NODE, COLS), BF16),
            jax.ShapeDtypeStruct((NODE, COLS), BF16),
            jax.ShapeDtypeStruct((NG, NZ, 2, PAD, 128), BF16),
            jax.ShapeDtypeStruct((NG, NZ, PAD, 128), BF16),
        ],
        in_specs=[anywhere] * 7,
        out_specs=[anywhere] * 4,
        scratch_shapes=[
            b(NODE, COLS),
            b(NODE, COLS),
            b(NG, NZ, 2, PAD, 128),
            b(NG, NZ, PAD, 128),
            b(NODE, 128, WIDTH),
            b(WIDTH, 3 * COLS),
            b(WIDTH, 3 * COLS),
            b(TEXTS * 128, 3 * COLS),
            b(COLS, WIDTH),
            b(COLS, WIDTH),
            b(COLS, WIDTH),
            pltpu.VMEM(ids.shape, jnp.int32),
            b(NODE, COLS),
            f(NODE, COLS),
            f(NODE, COLS),
            b(PAD, COLS),
            blocks,
            b(2 * PAD, DP * SLOT),
            b(DP * SLOT, 128),
            f(PAD, COLS),
            blocks,
            b(DP * SLOT, 128),
            blocks,
            blocks,
            blocks,
            blocks,
            blocks,
            blocks,
            b(2 * PAD, DP * SLOT),
            f(MP, NODE, COLS),
            f(MP, NODE, COLS),
            b(MP, PAD, COLS),
            b(2 * NODE, WIDTH // 2),
            b(MP, 2 * NODE, WIDTH // 2),
            f(PAD, WIDTH),
            b(128, 128),
            b(128, 128),
            b(NG, PAD, COLS),
            b(NG, PAD, COLS),
            b(NG, PAD, COLS),
            b(NG, PAD, COLS),
            b(NG, PAD, 128),
            b(NG, PAD, 128),
            b(2, 2, PAD, 128),
            b(NG, 2, PAD, 128),
            b(NZ, 2, PAD, 128),
            b(NZ, 2, PAD, 128),
            b(NZ, PAD, 128),
            b(NZ, PAD, 128),
            pltpu.SemaphoreType.DMA((NODE // TEXTS,)),
            pltpu.SemaphoreType.DMA((6,)),
            pltpu.SemaphoreType.DMA((4,)),
            pltpu.SemaphoreType.DMA((15,)),
            pltpu.SemaphoreType.DMA((15,)),
            pltpu.SemaphoreType.DMA((2, NZ)),
            pltpu.SemaphoreType.DMA((2, NZ)),
            pltpu.SemaphoreType.DMA((2, NY)),
            pltpu.SemaphoreType.DMA((2, NY)),
            pltpu.SemaphoreType.DMA((2, NY)),
            pltpu.SemaphoreType.DMA((2, NY)),
        ],
        compiler_params=pltpu.CompilerParams(
            collective_id=0, has_side_effects=True, vmem_limit_bytes=VMEM_LIMIT
        ),
        cost_estimate=pl.CostEstimate(flops=7 * 10**9, bytes_accessed=12 * 10**6, transcendentals=1600000),
    )(texts, w_qkv, w_out, w_self, w_neigh, ids, cot)


def finish_kernel(mixed, ngrad, sn, out, o_mixed, o_ngrad, o_self, o_neigh, o_out, small, fin_sn, fin_out, wide, isem, sem):
    def load(k, src, dst):
        copy = pltpu.make_async_copy(src, dst, isem.at[k])
        copy.start()
        return copy

    def store(k, src, dst):
        copy = pltpu.make_async_copy(src, dst, sem.at[k])
        copy.start()
        return copy

    blocks = [
        (load(j, sn.at[j], fin_sn.at[j]), load(NG + j, out.at[j], fin_out.at[j])) for j in range(NG)
    ]
    loads = [load(2 * NG + k, src, small.at[k]) for k, src in enumerate((mixed, ngrad))]
    stores = []
    for j in range(NG):
        cols = pl.ds(j * 128, 128)
        for copy in blocks[j]:
            copy.wait()
        for k, dst in enumerate((o_self, o_neigh, o_out)):
            block = fin_sn[j, :, k] if k < 2 else fin_out[j]
            wide[k, :, cols] = block.reshape(COLS, 128).astype(F32)
            stores.append(store(3 * j + k, wide.at[k, :, cols], dst.at[:, cols]))
    for k, dst in enumerate((o_mixed, o_ngrad)):
        loads[k].wait()
        stores.append(store(3 * NG + k, small.at[k], dst))
    for copy in stores:
        copy.wait()


def finish(mixed, ngrad, fin_sn, fin_out):
    anywhere = pl.BlockSpec(memory_space=pl.ANY)
    return pl.pallas_call(
        finish_kernel,
        out_shape=[
            jax.ShapeDtypeStruct((NODE, COLS), BF16),
            jax.ShapeDtypeStruct((NODE, COLS), BF16),
            jax.ShapeDtypeStruct((COLS, WIDTH), F32),
            jax.ShapeDtypeStruct((COLS, WIDTH), F32),
            jax.ShapeDtypeStruct((COLS, WIDTH), F32),
        ],
        in_specs=[anywhere] * 4,
        out_specs=[anywhere] * 5,
        scratch_shapes=[
            pltpu.VMEM((2, NODE, COLS), BF16),
            pltpu.VMEM((NG, NZ, 2, PAD, 128), BF16),
            pltpu.VMEM((NG, NZ, PAD, 128), BF16),
            pltpu.VMEM((3, COLS, WIDTH), F32),
            pltpu.SemaphoreType.DMA((2 * NG + 2,)),
            pltpu.SemaphoreType.DMA((3 * NG + 2,)),
        ],
        compiler_params=pltpu.CompilerParams(vmem_limit_bytes=VMEM_LIMIT),
        cost_estimate=pl.CostEstimate(flops=0, bytes_accessed=5 * 10**6, transcendentals=0),
    )(mixed, ngrad, fin_sn, fin_out)


def per_device(texts, w_qkv, w_out, w_self, w_neigh, neighbours, cotangent):
    return tuple(finish(*step(texts, w_qkv, w_out, w_self, w_neigh, neighbours.T, cotangent)))


def solution(mesh):
    return jax.shard_map(
        per_device,
        mesh=mesh,
        in_specs=(
            P("dp", None, None),
            P(None, "mp"),
            P("mp", None),
            P("mp", None),
            P("mp", None),
            P("dp", None),
            P("dp", "mp"),
        ),
        out_specs=(P("dp", "mp"), P("dp", "mp"), P("mp", None), P("mp", None), P("mp", None)),
        check_vma=False,
    )
```

```python
import math

import jax
import jax.numpy as jnp
from jax import lax
from jax.experimental import pallas as pl
from jax.experimental.pallas import tpu as pltpu
from jax.sharding import PartitionSpec as P

MESH = pl.DeviceIdType.MESH
F32, BF16 = jnp.float32, jnp.bfloat16
HD = 64
NODE = 24
PAD = 32
DP, MP, NZ, NG, NY = 64, 4, 8, 8, 4
COLS, WIDTH = 256, 1024
SLOT = 16
EMPTY = 120.0
MP_ORDER = (2, 1, 3)
GROUP_ORDER = (4, 5, 3, 2, 6, 7, 1)
FAR_FIRST = (4, 3, 5, 2, 6, 1, 7, 0)
VMEM_LIMIT = 60 * 2**20
TEXTS = 8


def dot(a, b):
    return jnp.dot(a, b, preferred_element_type=F32)


def dot_nt(a, b):
    return lax.dot_general(a, b, (((1,), (1,)), ((), ())), preferred_element_type=F32)


def dot_tn(a, b):
    return lax.dot_general(a, b, (((0,), (0,)), ((), ())), preferred_element_type=F32)


def iota(shape, dim):
    return lax.broadcasted_iota(jnp.int32, shape, dim)


def pad_rows(x, rows):
    return jnp.concatenate([x, jnp.zeros((rows - x.shape[0], x.shape[1]), x.dtype)], axis=0)


def request_names(ids_ref, want, spots_ref):
    ids = jnp.transpose(ids_ref[...].astype(F32))
    own = jnp.floor((ids + 0.5) * (1.0 / NODE))
    loc = ids - NODE * own
    live = ids >= 0.0
    fan = ids.shape[1]
    groups = iota((NODE, DP), 1).astype(F32)
    hots = [(own[:, f : f + 1] == groups).astype(F32) for f in range(fan)]
    total = hots[0]
    for f in range(1, fan):
        total = total + hots[f]
    lower = (iota((NODE, NODE), 1) < iota((NODE, NODE), 0)).astype(BF16)
    run = dot(lower, total.astype(BF16))
    lanes = iota((NODE, 128), 1).astype(F32)
    places, asks = [], []
    for f in range(fan):
        rank = jnp.sum(hots[f] * run, axis=1, keepdims=True)
        run = run + hots[f]
        places.append(jnp.where(live[:, f : f + 1], own[:, f : f + 1] * SLOT + rank, -1000.0))
        asks.append(jnp.where(lanes == rank, loc[:, f : f + 1] - EMPTY, 0.0))
    spots_ref[...] = jnp.concatenate(places, axis=1)
    owners = jnp.concatenate(hots, axis=0).astype(BF16)
    want[...] = dot_tn(owners, jnp.concatenate(asks, axis=0).astype(BF16)) + EMPTY


def routing(spots_ref, gh, ght, cnt_out):
    at = spots_ref[...]
    live = (at >= 0.0).astype(F32)
    cnt = jnp.maximum(jnp.sum(live, axis=1, keepdims=True), 1.0)
    cnt_out[...] = jnp.concatenate(
        [jnp.broadcast_to(cnt, (NODE, COLS)), jnp.ones((PAD - NODE, COLS), F32)], axis=0
    )
    spots = iota((NODE, DP * SLOT), 1).astype(F32)
    left = jnp.zeros((NODE, DP * SLOT), F32)
    right = jnp.zeros((NODE, DP * SLOT), F32)
    for f in range(at.shape[1]):
        left = jnp.where(spots == at[:, f : f + 1], 1.0, left)
        right = jnp.where(spots == at[:, f : f + 1] + 8.0, 1.0, right)
    gap = jnp.zeros((PAD - NODE, DP * SLOT), F32)
    both = jnp.concatenate([left, gap, right, gap], axis=0)
    gh[...] = both.astype(BF16)
    ght[...] = jnp.transpose(pad_rows(both, 128)).astype(BF16)


def order_columns(w, wp):
    low = iota((1, 128), 1) < HD
    for pair in range(2):
        base = pair * 384
        at = pair * 128
        a = w[:, base : base + 128].astype(F32)
        b = w[:, base + 128 : base + 256].astype(F32)
        c = w[:, base + 256 : base + 384].astype(F32)
        wp[:, at : at + 128] = jnp.where(low, a, b).astype(BF16)
        wp[:, 256 + at : 384 + at] = pltpu.roll(jnp.where(low, c, a), HD, 1).astype(BF16)
        wp[:, 512 + at : 640 + at] = jnp.where(low, b, c).astype(BF16)


def attend(qkv):
    low = iota((1, 128), 1) < HD
    scale = 1.0 / (math.sqrt(HD) * math.log(2.0))
    zero = jnp.zeros((), BF16)
    texts = []
    for t in range(TEXTS):
        rows = slice(t * 128, t * 128 + 128)
        parts = []
        for pair in range(2):
            at = pair * 128
            qt = qkv[rows, at : at + 128]
            kt = qkv[rows, 256 + at : 384 + at]
            vt = qkv[rows, 512 + at : 640 + at].astype(F32)
            two = jnp.concatenate([jnp.where(low, qt, zero), jnp.where(low, zero, qt)], axis=0)
            s = dot_nt(kt, two)
            e = jnp.exp2((s - jnp.max(s, axis=0, keepdims=True)) * scale)
            p = (e * (1.0 / jnp.sum(e, axis=0, keepdims=True))).astype(BF16).astype(F32)
            first = jnp.sum(p[:, :128], axis=1, keepdims=True)
            second = jnp.sum(p[:, 128:], axis=1, keepdims=True)
            parts.append(jnp.sum(jnp.where(low, first, second) * vt, axis=0, keepdims=True))
        texts.append(jnp.concatenate(parts, axis=1))
    return jnp.concatenate(texts, axis=0) * (1.0 / 128)


ASK, POOL_SUM, ROWS, POOL_ROWS, EMB_G, POOL_G, AGG_G, AGP_G, Z_ALL, COT, DZ_G, BACK, FACT = range(13)
SN_RS, OUT_RS = range(13, 15)


def step_kernel(
    texts_in, qkv_in, out_in, self_in, neigh_in, ids_in, cot_in,
    o_mixed, o_ngrad, o_sn, o_out,
    mixed, ngrad, fin_sn, fin_out, tx, wq, wp, qkv, w_out, w_self, w_neigh, ids, cot, acc, tmean, pooled, want, spots, gh, ght, cnt,
    asked, sel, sbufp, rbufp, sbuf, rbuf, sbuf2, rbuf2, sel_t, part, sums, cots, zsend, zall, full, e2, m2,
    emb_g, pool_g, agg_g, agp_g, dz2, dz_g, fact, fact_g, sn_s, sn_r, out_s, out_r,
    tsem, lsem, osem, ssem, rsem, z_s, z_r, y_s, y_r, c_s, c_r,
):
    m, d = lax.axis_index("mp"), lax.axis_index("dp")
    z, g = d // NG, d % NG
    y, c = g // 2, g % 2
    is_diag = (g // 2) == m

    def send(src, dst, phase, dp, mp):
        pltpu.make_async_remote_copy(
            src_ref=src, dst_ref=dst, send_sem=ssem.at[phase], recv_sem=rsem.at[phase],
            device_id=(dp, mp), device_id_type=MESH,
        ).start()

    def got(ref, phase):
        pltpu.make_async_copy(ref, ref, rsem.at[phase]).wait()

    def sent(ref, phase):
        pltpu.make_async_copy(ref, ref, ssem.at[phase]).wait()

    pending = []

    def emit(k, src, dst):
        copy = pltpu.make_async_copy(src, dst, osem.at[k])
        copy.start()
        pending.append(copy.wait)

    def later(ref, phase):
        pending.append(lambda: sent(ref, phase))

    def over(count, body):
        def step(i, carry):
            body(i)
            return carry

        lax.fori_loop(1, count, step, 0)

    def to_dp(src, dst, phase, offsets=FAR_FIRST):
        for k in offsets:

            def one(i, carry):
                to = ((z + k) % NZ) * NG + (g + i) % NG
                send(src.at[to], dst.at[d], phase, to, m)
                return carry

            lax.fori_loop(1 if k == 0 else 0, NG, one, 0)
        if offsets[-1] == 0:
            dst[d] = src[d]
            later(dst.at[pl.ds(0, DP - 1)], phase)

    def to_mp(src, dst, phase):
        for i in MP_ORDER:
            to = (m + i) % MP
            send(src.at[to], dst.at[m], phase, d, to)
        dst[m] = src[m]
        later(dst.at[pl.ds(0, MP - 1)], phase)

    def share_mp(src, dst, phase):
        for i in MP_ORDER:
            send(src, dst.at[m], phase, d, (m + i) % MP)
        later(dst.at[pl.ds(0, MP - 1)], phase)

    def to_group(block, phase):
        for i in GROUP_ORDER:
            send(block.at[g], block.at[g], phase, z * NG + (g + i) % NG, m)
        later(block.at[pl.ds(0, NG - 1)], phase)

    def to_columns(src, dst, phase):
        def one(i, carry):
            mp, half = i // 2, i % 2
            at = 2 * m + half
            here = jnp.logical_and(mp == m, at == g)

            @pl.when(jnp.logical_not(here))
            def _():
                send(src.at[half], dst.at[g], phase, z * NG + at, mp)

            @pl.when(here)
            def _():
                dst[g] = src[half]

            return carry

        lax.fori_loop(0, 2 * MP, one, 0)
        pending.append(lambda: sent_columns(dst, phase))

    def got_columns(dst, phase):
        @pl.when(is_diag)
        def _():
            got(dst.at[pl.ds(0, NG - 1)], phase)

        @pl.when(jnp.logical_not(is_diag))
        def _():
            got(dst, phase)

    def sent_columns(dst, phase):
        @pl.when(is_diag)
        def _():
            sent(dst.at[pl.ds(0, NG - 1)], phase)

        @pl.when(jnp.logical_not(is_diag))
        def _():
            sent(dst, phase)

    def scatter_z(src, dst, phase):
        for i in FAR_FIRST[:-1]:
            to = (z + i) % NZ
            send(src.at[to], dst.at[z], phase, to * NG + g, m)
        dst[z] = src[z]
        later(dst.at[pl.ds(0, NZ - 1)], phase)

    def z_copy(fin, at, to, k, which):
        return pltpu.make_async_remote_copy(
            src_ref=fin.at[g, at], dst_ref=fin.at[g, at], send_sem=z_s.at[which, k], recv_sem=z_r.at[which, k],
            device_id=(to * NG + g, m), device_id_type=MESH,
        )

    def along_y(fin, at, which):
        for i in MP_ORDER:
            pltpu.make_async_remote_copy(
                src_ref=fin.at[g, at], dst_ref=fin.at[g, at], send_sem=y_s.at[which, i], recv_sem=y_r.at[which, i],
                device_id=(z * NG + ((y + i) % NY) * 2 + c, m), device_id_type=MESH,
            ).start()

    def c_copy(fin, at, k, which):
        return pltpu.make_async_remote_copy(
            src_ref=fin.at[at], dst_ref=fin.at[at], send_sem=c_s.at[which, k], recv_sem=c_r.at[which, k],
            device_id=(z * NG + y * 2 + 1 - c, m), device_id_type=MESH,
        )

    def start_gather(fin, which):
        for k in FAR_FIRST[:-1]:
            copy = z_copy(fin, z, (z + k) % NZ, k, which)
            copy.start()
            pending.append(copy.wait_send)
        along_y(fin, z, which)

    def pass_along_y(fin, which):
        for k in reversed(FAR_FIRST[:-1]):
            at = (z + NZ - k) % NZ
            z_copy(fin, at, z, k, which).wait_recv()
            along_y(fin, at, which)
        own = c_copy(fin, g, 0, which)
        own.start()
        pending.append(own.wait_send)
        for i in range(1, NY):
            pending.append(pltpu.make_async_copy(fin.at[g], fin.at[g], y_s.at[which, i]).wait)

    def pass_to_core(fin, which):
        for i in range(1, NY):
            at = ((y + NY - i) % NY) * 2 + c
            pltpu.make_async_copy(fin.at[at], fin.at[at], y_r.at[which, i]).wait()
            copy = c_copy(fin, at, i, which)
            copy.start()
            pending.append(copy.wait_send)

    def end_gather(fin, which):
        for i in range(NY):
            c_copy(fin, ((y + NY - i) % NY) * 2 + 1 - c, i, which).wait_recv()

    weight = pltpu.make_async_copy(qkv_in, wq, lsem.at[0])
    names_in = pltpu.make_async_copy(ids_in, ids, lsem.at[1])
    names_in.start()
    weight.start()
    chunks = NODE // TEXTS

    def chunk(i):
        rows = pl.ds(i * TEXTS, TEXTS)
        return pltpu.make_async_copy(texts_in.at[rows], tx.at[rows], tsem.at[i])

    for i in range(chunks):
        chunk(i).start()
    others = [
        pltpu.make_async_copy(src, dst, lsem.at[2 + i])
        for i, (src, dst) in enumerate(
            [(out_in, w_out), (self_in, w_self), (neigh_in, w_neigh), (cot_in, cot)]
        )
    ]
    for copy in others:
        copy.start()

    bar = pltpu.get_barrier_semaphore()
    over(DP, lambda i: pl.semaphore_signal(bar, inc=1, device_id=((d + i) % DP, m), device_id_type=MESH))
    for i in range(1, MP):
        pl.semaphore_signal(bar, inc=1, device_id=(d, (m + i) % MP), device_id_type=MESH)

    def greet(i, carry):
        @pl.when(jnp.logical_not(jnp.logical_and(is_diag, i == g)))
        def _():
            pl.semaphore_signal(bar, inc=1, device_id=(z * NG + i, g // 2), device_id_type=MESH)

        return carry

    lax.fori_loop(0, NG, greet, 0)

    names_in.wait()
    request_names(ids, want, spots)
    e2[...] = jnp.zeros_like(e2)
    m2[...] = jnp.zeros_like(m2)
    weight.wait()
    order_columns(wq, wp)

    def work(i, carry):
        chunk(i).wait()
        rows = pl.ds(pl.multiple_of(i * TEXTS, TEXTS), TEXTS)
        qkv[...] = dot(tx[rows].reshape(TEXTS * 128, WIDTH), wp[...]).astype(BF16)
        acc[rows, :] = attend(qkv)
        mine = tx[rows, :, pl.ds(pl.multiple_of(m * COLS, COLS), COLS)]
        tmean[rows, :] = jnp.sum(mine.astype(F32), axis=1) * (1.0 / 128)

        @pl.when(i == 0)
        def _():
            pl.semaphore_wait(bar, DP - 1 + MP - 1 + 2 * MP - is_diag.astype(jnp.int32))
            for k in FAR_FIRST:

                def ask(j, none):
                    to = ((z + k) % NZ) * NG + (g + j) % NG
                    send(want.at[pl.ds(to, 1)], asked.at[pl.ds(d, 1)], ASK, to, m)
                    return none

                lax.fori_loop(1 if k == 0 else 0, NG, ask, 0)
            asked[pl.ds(d, 1), :] = want[pl.ds(d, 1), :]


        return carry

    lax.fori_loop(0, chunks, work, 0)
    for copy in others:
        copy.wait()
    pooled[...] = pad_rows(acc[...], PAD).astype(BF16)
    pool_g[g] = pooled[...]
    first = dot(pooled[...], w_out[...])
    for j in range(MP):
        part[j] = first[:NODE, j * COLS : (j + 1) * COLS]

    def halves(dst, x):
        dst[0:PAD, :] = x[:, :128]
        dst[PAD : 2 * PAD, :] = x[:, 128:]

    def whole(x):
        return jnp.concatenate([x[:PAD], x[PAD : 2 * PAD]], axis=1)

    def rows_of(onehot, x):
        return dot(onehot, x).astype(BF16).reshape(DP, SLOT, 128)

    to_mp(part, sums, POOL_SUM)
    cots[m] = pad_rows(cot[...], PAD)
    share_mp(cots.at[m], cots, COT)
    got(asked.at[pl.ds(0, DP - 1)], ASK)
    later(asked.at[pl.ds(0, DP - 1)], ASK)
    row = iota((DP * SLOT, 1), 0)
    block = (jnp.right_shift(row, 4) == iota((DP * SLOT, DP), 1)).astype(BF16)
    lane = iota((DP * SLOT, 128), 1)
    of_rank = jnp.where(lane == jnp.bitwise_and(row, 7), dot(block, asked[...].astype(BF16)), 0.0)
    names = jnp.sum(of_rank, axis=1, keepdims=True) + (PAD / 8) * jnp.bitwise_and(row, 8).astype(F32)
    hot = (names == lane.astype(F32)).astype(F32)
    sel[...] = hot.astype(BF16)
    halves(m2, pooled[...])
    sbufp[...] = rows_of(sel[...], m2[...])
    sel_t[...] = jnp.transpose(hot)[: 2 * PAD].astype(BF16)
    routing(spots, gh, ght, cnt)
    got(sums.at[pl.ds(0, MP - 1)], POOL_SUM)
    embed = tmean[...] + (sums[0] + sums[1] + sums[2] + sums[3])
    embed = pad_rows(embed, PAD).astype(BF16)
    halves(e2, embed)
    emb_g[g] = embed

    sbuf[...] = rows_of(sel[...], e2[...])
    to_dp(sbuf, rbuf, ROWS)
    to_dp(sbufp, rbufp, POOL_ROWS)
    zself = dot(embed, w_self[...])
    to_group(emb_g, EMB_G)
    to_group(pool_g, POOL_G)
    got(rbuf.at[pl.ds(0, DP - 1)], ROWS)
    agg = (whole(dot(gh[...], rbuf[...].reshape(DP * SLOT, 128))) / cnt[...]).astype(BF16)
    zfull = zself + dot(agg, w_neigh[...])
    zsend[...] = jnp.concatenate([zfull[:NODE, : WIDTH // 2], zfull[:NODE, WIDTH // 2 :]], axis=0).astype(BF16)
    share_mp(zsend, zall, Z_ALL)
    zall[m] = jnp.zeros((2 * NODE, WIDTH // 2), BF16)
    agg_g[g] = agg
    to_group(agg_g, AGG_G)
    got(rbufp.at[pl.ds(0, DP - 1)], POOL_ROWS)
    agp_g[g] = whole(dot(gh[...], rbufp[...].reshape(DP * SLOT, 128))).astype(BF16)
    to_group(agp_g, AGP_G)


    got(cots.at[pl.ds(0, MP - 1)], COT)
    got(zall.at[pl.ds(0, MP - 1)], Z_ALL)
    total = zall[0].astype(F32)
    for j in range(1, MP):
        total = total + zall[j].astype(F32)
    zc = zfull + pad_rows(jnp.concatenate([total[:NODE], total[NODE:]], axis=1), PAD)

    root = math.sqrt(2.0 / math.pi)
    th = jnp.tanh(root * (zc + 0.044715 * (zc * zc * zc)))
    cdf = 0.5 * (1.0 + th)
    slope = cdf + zc * (0.5 * (1.0 - th * th) * (root * (1.0 + (3 * 0.044715) * (zc * zc))))
    dz = (jnp.concatenate([cots[j] for j in range(MP)], axis=1).astype(F32) * slope).astype(BF16)
    for j in range(NG):
        dz2[j] = dz[:, j * 128 : j * 128 + 128]
    for i in GROUP_ORDER:
        to = (g + i) % NG
        send(dz2.at[to], dz_g.at[g], DZ_G, z * NG + to, m)
    dz_g[g] = dz2[g]
    later(dz_g.at[pl.ds(0, NG - 1)], DZ_G)

    own = dot_nt(dz, w_self[...])
    msg = (dot_nt(dz, w_neigh[...]) / cnt[...]).astype(BF16)
    for k, x in enumerate((own.astype(BF16), msg)):
        fact[0, k] = x[:, :128]
        fact[1, k] = x[:, 128:]
    to_columns(fact, fact_g, FACT)
    halves(m2, msg)
    sbuf2[...] = rows_of(ght[...], m2[...])
    to_dp(sbuf2, rbuf2, BACK)
    full[...] = zc * cdf
    mixed[...] = full[:NODE, pl.ds(pl.multiple_of(m * COLS, COLS), COLS)].astype(BF16)
    emit(0, mixed, o_mixed)

    def grad_of(lhs, rhs):
        return dot_tn(lhs[...].reshape(NG * PAD, COLS), rhs.reshape(NG * PAD, 128))

    def rounded(x):
        return x.astype(BF16).reshape(NZ, PAD, 128)

    got(dz_g.at[pl.ds(0, NG - 1)], DZ_G)
    got(emb_g.at[pl.ds(0, NG - 1)], EMB_G)
    got(agg_g.at[pl.ds(0, NG - 1)], AGG_G)
    sn_s[:, 0] = rounded(grad_of(emb_g, dz_g[...]))
    sn_s[:, 1] = rounded(grad_of(agg_g, dz_g[...]))
    scatter_z(sn_s, sn_r, SN_RS)

    factor = 1.0 / math.sqrt(NODE * DP)

    def z_total(buf):
        total = buf[0].astype(F32)
        for i in range(1, NZ):
            total = total + buf[i].astype(F32)
        return (total * factor).astype(BF16)

    got(pool_g.at[pl.ds(0, NG - 1)], POOL_G)
    got(agp_g.at[pl.ds(0, NG - 1)], AGP_G)
    got_columns(fact_g, FACT)
    out_s[...] = rounded(grad_of(pool_g, fact_g[:, 0]) + grad_of(agp_g, fact_g[:, 1]))
    scatter_z(out_s, out_r, OUT_RS)
    got(sn_r.at[pl.ds(0, NZ - 1)], SN_RS)
    fin_sn[g, z] = z_total(sn_r)
    start_gather(fin_sn, 0)

    got(out_r.at[pl.ds(0, NZ - 1)], OUT_RS)
    fin_out[g, z] = z_total(out_r)
    start_gather(fin_out, 1)
    pass_along_y(fin_sn, 0)
    pass_along_y(fin_out, 1)
    pass_to_core(fin_sn, 0)

    got(rbuf2.at[pl.ds(0, DP - 1)], BACK)
    grad = own + whole(dot(sel_t[...], rbuf2[...].reshape(DP * SLOT, 128)))
    ngrad[...] = grad[:NODE].astype(BF16)
    emit(1, ngrad, o_ngrad)
    end_gather(fin_sn, 0)
    emit(2, fin_sn, o_sn)
    pass_to_core(fin_out, 1)
    end_gather(fin_out, 1)
    emit(3, fin_out, o_out)

    for wait in pending:
        wait()


def step(texts, w_qkv, w_out, w_self, w_neigh, ids, cot):
    anywhere = pl.BlockSpec(memory_space=pl.ANY)
    b, f = (lambda *shape: pltpu.VMEM(shape, BF16)), (lambda *shape: pltpu.VMEM(shape, F32))
    blocks = b(DP, SLOT, 128)
    return pl.pallas_call(
        step_kernel,
        out_shape=[
            jax.ShapeDtypeStruct((NODE, COLS), BF16),
            jax.ShapeDtypeStruct((NODE, COLS), BF16),
            jax.ShapeDtypeStruct((NG, NZ, 2, PAD, 128), BF16),
            jax.ShapeDtypeStruct((NG, NZ, PAD, 128), BF16),
        ],
        in_specs=[anywhere] * 7,
        out_specs=[anywhere] * 4,
        scratch_shapes=[
            b(NODE, COLS),
            b(NODE, COLS),
            b(NG, NZ, 2, PAD, 128),
            b(NG, NZ, PAD, 128),
            b(NODE, 128, WIDTH),
            b(WIDTH, 3 * COLS),
            b(WIDTH, 3 * COLS),
            b(TEXTS * 128, 3 * COLS),
            b(COLS, WIDTH),
            b(COLS, WIDTH),
            b(COLS, WIDTH),
            pltpu.VMEM(ids.shape, jnp.int32),
            b(NODE, COLS),
            f(NODE, COLS),
            f(NODE, COLS),
            b(PAD, COLS),
            f(DP, 128),
            f(NODE, ids.shape[0]),
            b(2 * PAD, DP * SLOT),
            b(DP * SLOT, 128),
            f(PAD, COLS),
            f(DP, 128),
            b(DP * SLOT, 128),
            blocks,
            blocks,
            blocks,
            blocks,
            blocks,
            blocks,
            b(2 * PAD, DP * SLOT),
            f(MP, NODE, COLS),
            f(MP, NODE, COLS),
            b(MP, PAD, COLS),
            b(2 * NODE, WIDTH // 2),
            b(MP, 2 * NODE, WIDTH // 2),
            f(PAD, WIDTH),
            b(128, 128),
            b(128, 128),
            b(NG, PAD, COLS),
            b(NG, PAD, COLS),
            b(NG, PAD, COLS),
            b(NG, PAD, COLS),
            b(NG, PAD, 128),
            b(NG, PAD, 128),
            b(2, 2, PAD, 128),
            b(NG, 2, PAD, 128),
            b(NZ, 2, PAD, 128),
            b(NZ, 2, PAD, 128),
            b(NZ, PAD, 128),
            b(NZ, PAD, 128),
            pltpu.SemaphoreType.DMA((NODE // TEXTS,)),
            pltpu.SemaphoreType.DMA((6,)),
            pltpu.SemaphoreType.DMA((4,)),
            pltpu.SemaphoreType.DMA((15,)),
            pltpu.SemaphoreType.DMA((15,)),
            pltpu.SemaphoreType.DMA((2, NZ)),
            pltpu.SemaphoreType.DMA((2, NZ)),
            pltpu.SemaphoreType.DMA((2, NY)),
            pltpu.SemaphoreType.DMA((2, NY)),
            pltpu.SemaphoreType.DMA((2, NY)),
            pltpu.SemaphoreType.DMA((2, NY)),
        ],
        compiler_params=pltpu.CompilerParams(
            collective_id=0, has_side_effects=True, vmem_limit_bytes=VMEM_LIMIT
        ),
        cost_estimate=pl.CostEstimate(flops=7 * 10**9, bytes_accessed=12 * 10**6, transcendentals=1600000),
    )(texts, w_qkv, w_out, w_self, w_neigh, ids, cot)


def finish_kernel(mixed, ngrad, sn, out, o_mixed, o_ngrad, o_self, o_neigh, o_out, small, fin_sn, fin_out, wide, isem, sem):
    def load(k, src, dst):
        copy = pltpu.make_async_copy(src, dst, isem.at[k])
        copy.start()
        return copy

    def store(k, src, dst):
        copy = pltpu.make_async_copy(src, dst, sem.at[k])
        copy.start()
        return copy

    blocks = [
        (load(j, sn.at[j], fin_sn.at[j]), load(NG + j, out.at[j], fin_out.at[j])) for j in range(NG)
    ]
    loads = [load(2 * NG + k, src, small.at[k]) for k, src in enumerate((mixed, ngrad))]
    stores = []
    for j in range(NG):
        cols = pl.ds(j * 128, 128)
        for copy in blocks[j]:
            copy.wait()
        for k, dst in enumerate((o_self, o_neigh, o_out)):
            block = fin_sn[j, :, k] if k < 2 else fin_out[j]
            wide[k, :, cols] = block.reshape(COLS, 128).astype(F32)
            stores.append(store(3 * j + k, wide.at[k, :, cols], dst.at[:, cols]))
    for k, dst in enumerate((o_mixed, o_ngrad)):
        loads[k].wait()
        stores.append(store(3 * NG + k, small.at[k], dst))
    for copy in stores:
        copy.wait()


def finish(mixed, ngrad, fin_sn, fin_out):
    anywhere = pl.BlockSpec(memory_space=pl.ANY)
    return pl.pallas_call(
        finish_kernel,
        out_shape=[
            jax.ShapeDtypeStruct((NODE, COLS), BF16),
            jax.ShapeDtypeStruct((NODE, COLS), BF16),
            jax.ShapeDtypeStruct((COLS, WIDTH), F32),
            jax.ShapeDtypeStruct((COLS, WIDTH), F32),
            jax.ShapeDtypeStruct((COLS, WIDTH), F32),
        ],
        in_specs=[anywhere] * 4,
        out_specs=[anywhere] * 5,
        scratch_shapes=[
            pltpu.VMEM((2, NODE, COLS), BF16),
            pltpu.VMEM((NG, NZ, 2, PAD, 128), BF16),
            pltpu.VMEM((NG, NZ, PAD, 128), BF16),
            pltpu.VMEM((3, COLS, WIDTH), F32),
            pltpu.SemaphoreType.DMA((2 * NG + 2,)),
            pltpu.SemaphoreType.DMA((3 * NG + 2,)),
        ],
        compiler_params=pltpu.CompilerParams(vmem_limit_bytes=VMEM_LIMIT),
        cost_estimate=pl.CostEstimate(flops=0, bytes_accessed=5 * 10**6, transcendentals=0),
    )(mixed, ngrad, fin_sn, fin_out)


def per_device(texts, w_qkv, w_out, w_self, w_neigh, neighbours, cotangent):
    return tuple(finish(*step(texts, w_qkv, w_out, w_self, w_neigh, neighbours.T, cotangent)))


def solution(mesh):
    return jax.shard_map(
        per_device,
        mesh=mesh,
        in_specs=(
            P("dp", None, None),
            P(None, "mp"),
            P("mp", None),
            P("mp", None),
            P("mp", None),
            P("dp", None),
            P("dp", "mp"),
        ),
        out_specs=(P("dp", "mp"), P("dp", "mp"), P("mp", None), P("mp", None), P("mp", None)),
        check_vma=False,
    )
```
